1024 devices in a mesh: node: 128 (over z, x, core), local: 8 (over y).
Axes of the slice: x: 4, y: 8, z: 16, core: 2. Of those that a mesh axis runs over, the one named last changes fastest.
Arguments:
- hidden_in: bfloat16 [2048, 4096], P('node', 'local'), may hold values from -6 to 6
- grad_out: bfloat16 [2048, 4096], P('node', 'local'), may hold values from -0.59765625 to 0.59765625
- expert_ids: int32 [2048, 8], P('node'), may hold values from 0 to 127, as said below
- route_weights: float32 [2048, 8], P('node'), may hold values from 0.05 to 0.5
- gate_weight: bfloat16 [128, 4096, 1024], P('node', 'local'), may hold values from -0.09375 to 0.09375
- up_weight: bfloat16 [128, 4096, 1024], P('node', 'local'), may hold values from -0.09375 to 0.09375
- down_weight: bfloat16 [128, 1024, 4096], P('node', None, 'local'), may hold values from -0.1875 to 0.1875
Outputs:
- grad_in: bfloat16 [2048, 4096], P('node', 'local')
- grad_weights: bfloat16 [2048, 8], P('node')
The draws below stay inside these ranges and needn't reach their ends.
Inputs may be any that keep to these rules, and one draw needn't show every extreme that they name: `expert_ids`: expert e is held by node e; the experts form 8 groups of 16 consecutive numbers. Each token names 8 distinct experts, two in each of 4 distinct groups, and one group is named by every token of the same node. Within one node's block of 16 tokens no expert is named more than 2 times, and some expert exactly 2 times.
All inputs are finite; a program needn't handle non-finite values.
Results may differ from the reference program's by a relative error of at most 0.012.
Values may be sent and summed in bfloat16 or wider, within the bound.
No kernel may reach another device: no remote copies, remote signals or barrier semaphores. Data moves between devices by JAX's collectives and lax.ppermute only.
A program may use at most 32 MiB of HBM per device.

```python
import jax
import jax.numpy as jnp
from jax import lax

D = 4096
FF = 1024
TOP = 8
TOPG = 4
TOK_NODE = 16
EXPERTS = 128
GROUPS = 8
GS = 16
CAP = 2
ROWS = 256
TOKENS = 2048


def draw_expert_ids(key, part):
    key = jax.random.fold_in(key, 11)
    key_first, key_groups, key_rank, key_perm = jax.random.split(key, 4)
    node_count = TOKENS // TOK_NODE
    first = jax.random.randint(key_first, (node_count,), 0, GROUPS).astype(jnp.int32)
    group_iota = jnp.arange(GROUPS, dtype=jnp.int32)
    scores = jax.random.randint(key_groups, (node_count, TOK_NODE, GROUPS), 0, 2 ** 20).astype(jnp.int32) * GROUPS + group_iota
    scores = jnp.where(group_iota[None, None, :] == first[:, None, None], -1, scores)
    chosen = jnp.argsort(scores, axis=-1)[..., :TOPG].astype(jnp.int32)
    token_iota = jnp.arange(TOK_NODE, dtype=jnp.int32)
    rank_keys = jax.random.randint(key_rank, (node_count, TOK_NODE), 0, 2 ** 20).astype(jnp.int32) * TOK_NODE + token_iota
    ranks = jnp.argsort(rank_keys, axis=-1).astype(jnp.int32)
    place_iota = jnp.arange(GS, dtype=jnp.int32)
    perm_keys = jax.random.randint(key_perm, (node_count, GROUPS, GS), 0, 2 ** 20).astype(jnp.int32) * GS + place_iota
    perms = jnp.argsort(perm_keys, axis=-1).astype(jnp.int32)
    places = (2 * ranks[:, :, None, None] + jnp.arange(2, dtype=jnp.int32)[None, None, None, :]) % GS
    places = jnp.broadcast_to(places, (node_count, TOK_NODE, TOPG, 2)).astype(jnp.int32)
    spread = jnp.broadcast_to(perms[:, None, :, :], (node_count, TOK_NODE, GROUPS, GS))
    group_perm = jnp.take_along_axis(spread, chosen[..., None], axis=2)
    within = jnp.take_along_axis(group_perm, places, axis=3)
    experts = chosen[..., None] * GS + within
    return experts.reshape(TOKENS, TOP).astype(jnp.int32)


def levels(stream_key, shape, cuts, least, high):
    gain = 1.0
    for position, shards_of in cuts:
        heights = jax.random.uniform(jax.random.fold_in(jax.random.fold_in(stream_key, 6), position), (shards_of,), jnp.float32, least / len(cuts), high / len(cuts))
        gain = gain * jnp.repeat(jnp.exp(heights), shape[position] // shards_of).reshape((-1,) + (1,) * (len(shape) - 1 - position))
    return gain


def centred(key, dims, scale, most, shards=(), held_as=jnp.bfloat16):
    drawn = jax.random.normal(key, dims, jnp.float32) * scale
    if len(shards) > 0:
        drawn = levels(key, dims, shards, -0.22, 0.18) * drawn
    return jnp.clip(drawn, min=-most, max=most).astype(held_as)


def setup_inputs(seed: int = 0) -> dict:
    key_of = jax.random.split(jax.random.key(seed), 8)
    return {
        "hidden_in": centred(key_of[0], (TOKENS, D), 1.0, 6.0, ((0, 128), (1, 8))),
        "grad_out": centred(key_of[1], (TOKENS, D), 0.1, 0.59765625, ((0, 128), (1, 8))),
        "expert_ids": draw_expert_ids(jax.random.fold_in(key_of[7], 71), 0),
        "route_weights": jnp.clip(0.05 + 0.45 * jax.random.uniform(key_of[3], (TOKENS, TOP), jnp.float32) ** levels(key_of[3], (TOKENS, TOP), ((0, 128),), -0.2, 0.2), 0.05, 0.5),
        "gate_weight": centred(key_of[4], (EXPERTS, D, FF), D ** -0.5, 0.09375, ((0, 128), (1, 8))),
        "up_weight": centred(key_of[5], (EXPERTS, D, FF), D ** -0.5, 0.09375, ((0, 128), (1, 8))),
        "down_weight": centred(key_of[6], (EXPERTS, FF, D), FF ** -0.5, 0.1875, ((0, 128), (2, 8))),
    }


def contract_last(left, right):
    return lax.dot_general(left, right, (((1,), (1,)), ((), ())), preferred_element_type=jnp.float32)


def route_slots(expert_ids):
    blocks = expert_ids.reshape(-1, TOK_NODE, TOP)
    matches = blocks[:, :, :, None, None] == blocks[:, None, None, :, :]
    order = jnp.arange(TOK_NODE, dtype=jnp.int32)
    earlier = order[None, None, None, :, None] < order[None, :, None, None, None]
    counted = jnp.sum((matches & earlier).astype(jnp.int32), axis=(3, 4))
    return counted.reshape(TOKENS, TOP).astype(jnp.int32)


def hidden_grads(gate_pre, up_pre, grad_act):
    sig = jax.nn.sigmoid(gate_pre)
    silu_val = gate_pre * sig
    act = silu_val * up_pre
    score = jnp.sum(act * grad_act, axis=1)
    grad_gate = (grad_act * up_pre * sig * (1.0 + gate_pre * (1.0 - sig))).astype(jnp.bfloat16)
    grad_up = (grad_act * silu_val).astype(jnp.bfloat16)
    return grad_gate, grad_up, score


def reference(hidden_in, grad_out, expert_ids, route_weights, gate_weight, up_weight, down_weight):
    slot = route_slots(expert_ids)
    token_node = (jnp.arange(TOKENS, dtype=jnp.int32) // TOK_NODE)[:, None]
    slot_index = (token_node * CAP + slot).astype(jnp.int32)
    route_ids = jnp.arange(TOKENS * TOP, dtype=jnp.int32)
    table = jnp.full((EXPERTS, ROWS), TOKENS * TOP, jnp.int32)
    table = table.at[expert_ids.reshape(-1), slot_index.reshape(-1)].set(route_ids)
    x_pad = jnp.concatenate([hidden_in, jnp.zeros((1, D), hidden_in.dtype)], axis=0)
    y_pad = jnp.concatenate([grad_out, jnp.zeros((1, D), grad_out.dtype)], axis=0)
    w_pad = jnp.concatenate([route_weights.reshape(-1), jnp.zeros((1,), jnp.float32)])

    def expert_step(carry, inputs):
        grad_acc, score_acc = carry
        w_gate, w_up, w_down, routes = inputs
        token_rows = (routes // TOP).astype(jnp.int32)
        x_rows = x_pad[token_rows]
        y_rows = y_pad[token_rows]
        gate_pre = jnp.dot(x_rows, w_gate, preferred_element_type=jnp.float32)
        up_pre = jnp.dot(x_rows, w_up, preferred_element_type=jnp.float32)
        grad_act = contract_last(y_rows, w_down)
        grad_gate, grad_up, score = hidden_grads(gate_pre, up_pre, grad_act)
        expert_grad = (contract_last(grad_gate, w_gate) + contract_last(grad_up, w_up)).astype(jnp.bfloat16)
        scaled = w_pad[routes][:, None] * expert_grad.astype(jnp.float32)
        grad_acc = grad_acc.at[token_rows].add(scaled)
        score_acc = score_acc.at[routes].set(score.astype(jnp.bfloat16))
        return (grad_acc, score_acc), None

    start = (jnp.zeros((TOKENS + 1, D), jnp.float32), jnp.zeros((TOKENS * TOP + 1,), jnp.bfloat16))
    (grad_acc, score_acc), _ = lax.scan(expert_step, start, (gate_weight, up_weight, down_weight, table))
    grad_in = grad_acc[:TOKENS].astype(jnp.bfloat16)
    grad_weights = score_acc[:TOKENS * TOP].reshape(TOKENS, TOP)
    return grad_in, grad_weights
```

```python
import functools

import jax
import jax.numpy as jnp
from jax import lax
from jax.experimental import pallas as pl
from jax.experimental.pallas import tpu as pltpu
from jax.sharding import PartitionSpec as P

BF16 = jnp.bfloat16
F32 = jnp.float32
EMPTY = 64.0
LANES = 128
EXTRA = 16
PARAMS = pltpu.CompilerParams(vmem_limit_bytes=32 * 1024 * 1024)


def dot(left, right, left_dim=1, right_dim=0):
    return lax.dot_general(
        left, right, (((left_dim,), (right_dim,)), ((), ())), preferred_element_type=F32
    )


def iota(shape, dim):
    return lax.broadcasted_iota(jnp.int32, shape, dim)


def route_hits(ids, node_count, slot_cap):
    toks, routes = ids.shape
    experts = iota((toks, node_count), 1)
    named = jnp.zeros((toks, node_count), F32)
    for k in range(routes):
        named += (ids[:, k : k + 1] == experts).astype(F32)
    before = (iota((toks, toks), 1) < iota((toks, toks), 0)).astype(BF16)
    earlier = dot(before, named.astype(BF16))
    slots = iota((toks, node_count * slot_cap), 1)
    hits = []
    for k in range(routes):
        expert = ids[:, k : k + 1]
        slot = jnp.sum(jnp.where(expert == experts, earlier, 0.0), axis=1, keepdims=True)
        hits.append(slots == expert * slot_cap + slot.astype(jnp.int32))
    return hits


def dispatch_kernel(node_count, slot_cap, ids_ref, x_ref, y_ref, out_ref):
    toks = ids_ref.shape[0]
    hits = route_hits(ids_ref[...], node_count, slot_cap)
    taken = functools.reduce(jnp.logical_or, hits).astype(F32)
    free = 1.0 - jnp.sum(taken, axis=0, keepdims=True)
    free = jnp.where(iota(taken.shape, 0) == 0, jnp.broadcast_to(free, taken.shape), 0.0)
    pick = jnp.concatenate([taken, free], axis=0).astype(BF16)
    width = x_ref.shape[1]
    for place, ref in enumerate((x_ref, y_ref)):
        rows = jnp.concatenate([ref[...], jnp.full((toks, width), EMPTY, BF16)], axis=0)
        out_ref[:, place * width : (place + 1) * width] = dot(pick, rows, 0, 0).astype(BF16)


def parts_kernel(rows_ref, gate_ref, up_ref, down_ref, out_ref):
    parts = out_ref.shape[0]
    width = gate_ref.shape[0]
    x = rows_ref[:, :width]
    y = rows_ref[:, width:]
    for j in range(0, parts, 2):
        step = min(2, parts - j)
        cols = slice(j * LANES, (j + step) * LANES)
        products = (
            dot(x, gate_ref[:, cols]),
            dot(x, up_ref[:, cols]),
            dot(y, down_ref[cols, :], 1, 1),
        )
        for i in range(step):
            for place, value in enumerate(products):
                out_ref[j + i, :, place * LANES : (place + 1) * LANES] = value[
                    :, i * LANES : (i + 1) * LANES
                ].astype(BF16)


def hidden_kernel(parts_ref, out_ref):
    parts, rows, _ = parts_ref.shape
    total = parts_ref[0].astype(F32)
    for j in range(1, parts):
        total += parts_ref[j].astype(F32)
    gate_pre = total[:, :LANES]
    up_pre = total[:, LANES : 2 * LANES]
    grad_act = total[:, 2 * LANES :]
    sig = jax.nn.sigmoid(gate_pre)
    silu_val = gate_pre * sig
    product = silu_val * up_pre * grad_act
    grad_gate = (grad_act * up_pre * sig * (1.0 + gate_pre * (1.0 - sig))).astype(BF16)
    grad_up = (grad_act * silu_val).astype(BF16)
    score = lax.dot_general(
        jnp.ones((8, LANES), F32), product, (((1,), (1,)), ((), ())),
        preferred_element_type=F32, precision=lax.Precision.HIGHEST,
    )
    high = score.astype(BF16).astype(F32)
    tail = jnp.concatenate([high, score - high], axis=0).astype(BF16)
    pad = jnp.zeros((EXTRA, 2 * LANES - rows), BF16) if rows < 2 * LANES else None
    if pad is not None:
        tail = jnp.concatenate([tail, pad], axis=1)
    for j in range(parts):
        out_ref[j, :rows, :LANES] = grad_gate
        out_ref[j, :rows, LANES:] = grad_up
        out_ref[j, rows:, :] = tail


def back_kernel(hidden_ref, gate_ref, up_ref, out_ref):
    parts, rows, _ = hidden_ref.shape
    rows -= EXTRA
    width = gate_ref.shape[0]
    total = jnp.zeros((rows, width), F32)
    score = jnp.zeros((8, 2 * LANES), F32)
    for j in range(parts):
        cols = slice(j * LANES, (j + 1) * LANES)
        weights = jnp.concatenate([gate_ref[:, cols], up_ref[:, cols]], axis=1)
        total += dot(hidden_ref[j, :rows, :], weights, 1, 1)
        tail = hidden_ref[j, rows:, :].astype(F32)
        score += tail[:8] + tail[8:]
    out_ref[:, :width] = total.astype(BF16)
    score = score[:, :rows].astype(BF16)
    unit = (iota((rows, rows), 0) == iota((rows, rows), 1)).astype(BF16)
    spread = jnp.concatenate([score] * (LANES // 8), axis=0)
    out_ref[:, width:] = dot(unit, spread, 1, 1).astype(BF16)


def home_kernel(node_count, slot_cap, ids_ref, route_ref, back_ref, grad_ref, score_ref):
    width = grad_ref.shape[1]
    toks, routes = ids_ref.shape
    hits = route_hits(ids_ref[...], node_count, slot_cap)
    weight = jnp.zeros(hits[0].shape, F32)
    for k in range(routes):
        weight += jnp.where(hits[k], route_ref[:, k : k + 1], 0.0)
    high = weight.astype(BF16)
    rest = weight - high.astype(F32)
    middle = rest.astype(BF16)
    low = (rest - middle.astype(F32)).astype(BF16)
    split = jnp.concatenate([high, middle, low], axis=0)
    sums = dot(split, back_ref[:, :width])
    grad_ref[...] = (sums[:toks] + sums[toks : 2 * toks] + sums[2 * toks :]).astype(BF16)
    picks = jnp.concatenate([hit.astype(BF16) for hit in hits], axis=0)
    scores = dot(picks, back_ref[:, width:])
    lane = iota((toks, LANES), 1)
    placed = jnp.zeros((toks, LANES), F32)
    for k in range(routes):
        placed = jnp.where(lane == k, scores[k * toks : (k + 1) * toks], placed)
    score_ref[...] = placed[:, :routes].astype(BF16)


def on_device(hidden_in, grad_out, expert_ids, route_weights, gate_weight, up_weight, down_weight):
    node_count = lax.axis_size("node")
    parts = lax.axis_size("local")
    tok_count, width = hidden_in.shape
    group_count = min(8, node_count // 2)
    slot_cap = 2 * tok_count // (node_count // group_count)
    slot_total = node_count * slot_cap
    w_gate, w_up, w_down = gate_weight[0], up_weight[0], down_weight[0]

    def call(kernel, shape, *args):
        return pl.pallas_call(
            kernel,
            out_shape=jax.tree.map(lambda s: jax.ShapeDtypeStruct(s, BF16), shape, is_leaf=lambda s: isinstance(s, tuple) and isinstance(s[0], int)),
            compiler_params=PARAMS,
        )(*args)

    send = call(
        functools.partial(dispatch_kernel, node_count, slot_cap),
        (slot_total, 2 * width), expert_ids, hidden_in, grad_out,
    ).reshape(node_count, slot_cap, 2 * width)
    recv = lax.all_to_all(send, "node", split_axis=0, concat_axis=0, tiled=True)
    rows = recv.reshape(slot_total, 2 * width)
    sums = call(parts_kernel, (parts, slot_total, 3 * LANES), rows, w_gate, w_up, w_down)
    sums = lax.all_to_all(sums, "local", split_axis=0, concat_axis=0, tiled=True)
    hidden = call(hidden_kernel, (parts, slot_total + EXTRA, 2 * LANES), sums)
    hidden = lax.all_to_all(hidden, "local", split_axis=0, concat_axis=0, tiled=True)
    back = call(back_kernel, (slot_total, width + LANES), hidden, w_gate, w_up)
    back = back.reshape(node_count, slot_cap, width + LANES)
    home = lax.all_to_all(back, "node", split_axis=0, concat_axis=0, tiled=True)
    home = home.reshape(slot_total, width + LANES)
    grad_in, grad_weights = call(
        functools.partial(home_kernel, node_count, slot_cap),
        [(tok_count, width), (tok_count, expert_ids.shape[1])], expert_ids, route_weights, home,
    )
    return (grad_in, grad_weights)


def solution(mesh):
    return jax.shard_map(
        on_device,
        mesh=mesh,
        in_specs=(
            P("node", "local"),
            P("node", "local"),
            P("node", None),
            P("node", None),
            P("node", "local", None),
            P("node", "local", None),
            P("node", None, "local"),
        ),
        out_specs=(P("node", "local"), P("node", None)),
        check_vma=False,
    )
```

```python
import functools

import jax
import jax.numpy as jnp
from jax import lax
from jax.experimental import pallas as pl
from jax.experimental.pallas import tpu as pltpu
from jax.sharding import PartitionSpec as P

BF16 = jnp.bfloat16
F32 = jnp.float32
EMPTY = 64.0
LANES = 128
EXTRA = 16
PARAMS = pltpu.CompilerParams(vmem_limit_bytes=32 * 1024 * 1024)


def dot(left, right, left_dim=1, right_dim=0):
    return lax.dot_general(
        left, right, (((left_dim,), (right_dim,)), ((), ())), preferred_element_type=F32
    )


def iota(shape, dim):
    return lax.broadcasted_iota(jnp.int32, shape, dim)


def route_hits(ids, node_count, slot_cap):
    toks, routes = ids.shape
    experts = iota((toks, node_count), 1)
    named = jnp.zeros((toks, node_count), F32)
    for k in range(routes):
        named += (ids[:, k : k + 1] == experts).astype(F32)
    before = (iota((toks, toks), 1) < iota((toks, toks), 0)).astype(BF16)
    earlier = dot(before, named.astype(BF16))
    slots = iota((toks, node_count * slot_cap), 1)
    hits = []
    for k in range(routes):
        expert = ids[:, k : k + 1]
        slot = jnp.sum(jnp.where(expert == experts, earlier, 0.0), axis=1, keepdims=True)
        hits.append(slots == expert * slot_cap + slot.astype(jnp.int32))
    return hits


def dispatch_kernel(node_count, slot_cap, ids_ref, x_ref, y_ref, out_ref):
    toks = ids_ref.shape[0]
    hits = route_hits(ids_ref[...], node_count, slot_cap)
    taken = functools.reduce(jnp.logical_or, hits).astype(F32)
    free = 1.0 - jnp.sum(taken, axis=0, keepdims=True)
    free = jnp.where(iota(taken.shape, 0) == 0, jnp.broadcast_to(free, taken.shape), 0.0)
    pick = jnp.concatenate([taken, free], axis=0).astype(BF16)
    width = x_ref.shape[1]
    for place, ref in enumerate((x_ref, y_ref)):
        rows = jnp.concatenate([ref[...], jnp.full((toks, width), EMPTY, BF16)], axis=0)
        out_ref[:, place * width : (place + 1) * width] = dot(pick, rows, 0, 0).astype(BF16)


def parts_kernel(rows_ref, gate_ref, up_ref, down_ref, main_ref, rest_ref, place_ref, count_ref):
    parts, main, _ = main_ref.shape
    slots = rows_ref.shape[0]
    width = gate_ref.shape[0]
    named = rows_ref[:, :LANES].astype(F32)[:, :1] < 0.5 * EMPTY
    named_wide = jnp.broadcast_to(named.astype(F32), (slots, LANES))
    before = (iota((slots, slots), 1) < iota((slots, slots), 0)).astype(BF16)
    order = dot(before, named_wide.astype(BF16))[:, :1].astype(jnp.int32)
    place = (jnp.where(named, order, slots) == iota((slots, slots), 1)).astype(BF16)
    place_ref[...] = place
    count_ref[0, 0] = jnp.sum(named_wide[:, :1]).astype(jnp.int32)
    x = dot(place, rows_ref[:, :width], 0, 0).astype(BF16)
    y = dot(place, rows_ref[:, width:], 0, 0).astype(BF16)
    for j in range(0, parts, 2):
        step = min(2, parts - j)
        cols = slice(j * LANES, (j + step) * LANES)
        products = (
            dot(x, gate_ref[:, cols]),
            dot(x, up_ref[:, cols]),
            dot(y, down_ref[cols, :], 1, 1),
        )
        for i in range(step):
            for at, value in enumerate(products):
                piece = value[:, i * LANES : (i + 1) * LANES].astype(BF16)
                main_ref[j + i, :, at * LANES : (at + 1) * LANES] = piece[:main]
                rest_ref[j + i, :, at * LANES : (at + 1) * LANES] = piece[main:]


def hidden_kernel(parts_ref, out_ref):
    parts, rows, _ = parts_ref.shape
    total = parts_ref[0].astype(F32)
    for j in range(1, parts):
        total += parts_ref[j].astype(F32)
    gate_pre = total[:, :LANES]
    up_pre = total[:, LANES : 2 * LANES]
    grad_act = total[:, 2 * LANES :]
    sig = jax.nn.sigmoid(gate_pre)
    silu_val = gate_pre * sig
    product = silu_val * up_pre * grad_act
    grad_gate = (grad_act * up_pre * sig * (1.0 + gate_pre * (1.0 - sig))).astype(BF16)
    grad_up = (grad_act * silu_val).astype(BF16)
    score = lax.dot_general(
        jnp.ones((8, LANES), F32), product, (((1,), (1,)), ((), ())),
        preferred_element_type=F32, precision=lax.Precision.HIGHEST,
    )
    high = score.astype(BF16).astype(F32)
    tail = jnp.concatenate([high, score - high], axis=0).astype(BF16)
    pad = jnp.zeros((EXTRA, 2 * LANES - rows), BF16) if rows < 2 * LANES else None
    if pad is not None:
        tail = jnp.concatenate([tail, pad], axis=1)
    for j in range(parts):
        out_ref[j, :rows, :LANES] = grad_gate
        out_ref[j, :rows, LANES:] = grad_up
        out_ref[j, rows:, :] = tail


def back_rows(hidden_ref, gate_ref, up_ref):
    parts, rows, _ = hidden_ref.shape
    rows -= EXTRA
    width = gate_ref.shape[0]
    total = jnp.zeros((rows, width), F32)
    score = jnp.zeros((8, 2 * LANES), F32)
    for j in range(parts):
        cols = slice(j * LANES, (j + 1) * LANES)
        weights = jnp.concatenate([gate_ref[:, cols], up_ref[:, cols]], axis=1)
        total += dot(hidden_ref[j, :rows, :], weights, 1, 1)
        tail = hidden_ref[j, rows:, :].astype(F32)
        score += tail[:8] + tail[8:]
    score = score.astype(BF16)
    unit = (iota((rows, 2 * LANES), 0) == iota((rows, 2 * LANES), 1)).astype(BF16)
    spread = jnp.concatenate([score] * (LANES // 8), axis=0)
    return total.astype(BF16), dot(unit, spread, 1, 1).astype(BF16)


def rest_kernel(hidden_ref, gate_ref, up_ref, out_ref):
    width = gate_ref.shape[0]
    out_ref[:, :width], out_ref[:, width:] = back_rows(hidden_ref, gate_ref, up_ref)


def back_kernel(hidden_ref, gate_ref, up_ref, rest_ref, place_ref, out_ref):
    width = gate_ref.shape[0]
    main, main_score = back_rows(hidden_ref, gate_ref, up_ref)
    rows = jnp.concatenate([main, rest_ref[:, :width]], axis=0)
    out_ref[:, :width] = dot(place_ref[...], rows).astype(BF16)
    score = jnp.concatenate([main_score, rest_ref[:, width:]], axis=0)
    out_ref[:, width:] = dot(place_ref[...], score).astype(BF16)


def home_kernel(node_count, slot_cap, ids_ref, route_ref, back_ref, grad_ref, score_ref):
    width = grad_ref.shape[1]
    toks, routes = ids_ref.shape
    hits = route_hits(ids_ref[...], node_count, slot_cap)
    weight = jnp.zeros(hits[0].shape, F32)
    for k in range(routes):
        weight += jnp.where(hits[k], route_ref[:, k : k + 1], 0.0)
    high = weight.astype(BF16)
    rest = weight - high.astype(F32)
    middle = rest.astype(BF16)
    low = (rest - middle.astype(F32)).astype(BF16)
    split = jnp.concatenate([high, middle, low], axis=0)
    sums = dot(split, back_ref[:, :width])
    grad_ref[...] = (sums[:toks] + sums[toks : 2 * toks] + sums[2 * toks :]).astype(BF16)
    picks = jnp.concatenate([hit.astype(BF16) for hit in hits], axis=0)
    scores = dot(picks, back_ref[:, width:])
    lane = iota((toks, LANES), 1)
    placed = jnp.zeros((toks, LANES), F32)
    for k in range(routes):
        placed = jnp.where(lane == k, scores[k * toks : (k + 1) * toks], placed)
    score_ref[...] = placed[:, :routes].astype(BF16)


def on_device(hidden_in, grad_out, expert_ids, route_weights, gate_weight, up_weight, down_weight):
    node_count = lax.axis_size("node")
    parts = lax.axis_size("local")
    tok_count, width = hidden_in.shape
    group_count = min(8, node_count // 2)
    slot_cap = 2 * tok_count // (node_count // group_count)
    slot_total = node_count * slot_cap
    w_gate, w_up, w_down = gate_weight[0], up_weight[0], down_weight[0]

    def call(kernel, shape, *args):
        return pl.pallas_call(
            kernel,
            out_shape=jax.tree.map(lambda s: jax.ShapeDtypeStruct(s, BF16), shape, is_leaf=lambda s: isinstance(s, tuple) and isinstance(s[0], int)),
            compiler_params=PARAMS,
        )(*args)

    send = call(
        functools.partial(dispatch_kernel, node_count, slot_cap),
        (slot_total, 2 * width), expert_ids, hidden_in, grad_out,
    ).reshape(node_count, slot_cap, 2 * width)
    recv = lax.all_to_all(send, "node", split_axis=0, concat_axis=0, tiled=True)
    rows = recv.reshape(slot_total, 2 * width)
    main = max(EXTRA, slot_total * 5 // 8 // EXTRA * EXTRA)
    vmem = pl.BlockSpec(memory_space=pltpu.VMEM)
    main_sums, rest_sums, place, count = pl.pallas_call(
        parts_kernel,
        out_shape=[
            jax.ShapeDtypeStruct((parts, main, 3 * LANES), BF16),
            jax.ShapeDtypeStruct((parts, slot_total - main, 3 * LANES), BF16),
            jax.ShapeDtypeStruct((slot_total, slot_total), BF16),
            jax.ShapeDtypeStruct((1, 1), jnp.int32),
        ],
        out_specs=[vmem, vmem, vmem, pl.BlockSpec(memory_space=pltpu.SMEM)],
        compiler_params=PARAMS,
    )(rows, w_gate, w_up, w_down)

    def over_local(sums):
        sums = lax.all_to_all(sums, "local", split_axis=0, concat_axis=0, tiled=True)
        hidden = call(hidden_kernel, (parts, sums.shape[1] + EXTRA, 2 * LANES), sums)
        return lax.all_to_all(hidden, "local", split_axis=0, concat_axis=0, tiled=True)

    def rest_of(sums, w_gate, w_up):
        return call(rest_kernel, (slot_total - main, width + LANES), over_local(sums), w_gate, w_up)

    rest = lax.cond(
        count[0, 0] > main,
        rest_of,
        lambda *_: jnp.zeros((slot_total - main, width + LANES), BF16),
        rest_sums, w_gate, w_up,
    )
    hidden = over_local(main_sums)
    back = call(back_kernel, (slot_total, width + LANES), hidden, w_gate, w_up, rest, place)
    back = back.reshape(node_count, slot_cap, width + LANES)
    home = lax.all_to_all(back, "node", split_axis=0, concat_axis=0, tiled=True)
    home = home.reshape(slot_total, width + LANES)
    grad_in, grad_weights = call(
        functools.partial(home_kernel, node_count, slot_cap),
        [(tok_count, width), (tok_count, expert_ids.shape[1])], expert_ids, route_weights, home,
    )
    return (grad_in, grad_weights)


def solution(mesh):
    return jax.shard_map(
        on_device,
        mesh=mesh,
        in_specs=(
            P("node", "local"),
            P("node", "local"),
            P("node", None),
            P("node", None),
            P("node", "local", None),
            P("node", "local", None),
            P("node", None, "local"),
        ),
        out_specs=(P("node", "local"), P("node", None)),
        check_vma=False,
    )
```

```python
import functools

import jax
import jax.numpy as jnp
from jax import lax
from jax.experimental import pallas as pl
from jax.experimental.pallas import tpu as pltpu
from jax.sharding import PartitionSpec as P

BF16 = jnp.bfloat16
F32 = jnp.float32
EMPTY = 64.0
LANES = 128
EXTRA = 16
PARAMS = pltpu.CompilerParams(vmem_limit_bytes=32 * 1024 * 1024)


def dot(left, right, left_dim=1, right_dim=0):
    return lax.dot_general(
        left, right, (((left_dim,), (right_dim,)), ((), ())), preferred_element_type=F32
    )


def iota(shape, dim):
    return lax.broadcasted_iota(jnp.int32, shape, dim)


def split_three(value):
    high = value.astype(BF16)
    rest = value - high.astype(F32)
    middle = rest.astype(BF16)
    return high, middle, (rest - middle.astype(F32)).astype(BF16)


def pack_kernel(size, ids_in, route_in, x_in, y_in, out_ref, ids_ref, route_ref, x_ref, y_ref, sems):
    pairs = ((ids_in, ids_ref), (route_in, route_ref), (x_in, x_ref), (y_in, y_ref))
    copies = [pltpu.make_async_copy(*pair, sems.at[i]) for i, pair in enumerate(pairs)]
    for copy in copies:
        copy.start()
    for copy in copies:
        copy.wait()
    groups, toks, _ = out_ref.shape
    routes = ids_ref.shape[0]
    width = x_ref.shape[1]
    unit = (iota((toks, toks), 0) == iota((toks, toks), 1)).astype(BF16)
    pieces = [piece.astype(F32) for piece in split_three(route_ref[...])]
    fill = jnp.zeros((LANES - 4 * routes, toks), F32)
    for group in range(groups):
        ids = (ids_ref[...] - group * size).astype(F32)
        facts = jnp.concatenate([ids, *pieces, fill], axis=0).astype(BF16)
        out_ref[group, :, :width] = x_ref[...]
        out_ref[group, :, width : 2 * width] = y_ref[...]
        out_ref[group, :, 2 * width :] = dot(unit, facts, 1, 1).astype(BF16)


def route_hits(facts, groups, toks, size, slot_cap, routes):
    shape = (groups * toks, size * groups * slot_cap)
    column = iota(shape, 1)
    expert = column // (groups * slot_cap)
    names = [facts[:, k : k + 1].astype(jnp.int32) == expert for k in range(routes)]
    named = functools.reduce(jnp.logical_or, names)
    square = (groups * toks, groups * toks)
    one, two = iota(square, 0), iota(square, 1)
    before = ((one // toks == two // toks) & (two < one)).astype(BF16)
    earlier = dot(before, named.astype(BF16)).astype(jnp.int32)
    here = (earlier == column % slot_cap) & (
        column // slot_cap % groups == iota(shape, 0) // toks
    )
    return [name & here for name in names], named & here


def rows_kernel(routes, slot_cap, tok_ref, out_ref):
    groups, toks, full = tok_ref.shape
    size = out_ref.shape[0]
    width = full - LANES
    toks_all = tok_ref[...].reshape(groups * toks, full)
    facts = toks_all[:, width:].astype(F32)
    _, taken = route_hits(facts, groups, toks, size, slot_cap, routes)
    taken = taken.astype(F32)
    free = 1.0 - jnp.sum(taken, axis=0, keepdims=True)
    shape = (EXTRA, taken.shape[1])
    free = jnp.where(iota(shape, 0) == 0, jnp.broadcast_to(free, shape), 0.0)
    pick = jnp.concatenate([taken, free], axis=0).astype(BF16)
    rows = jnp.concatenate([toks_all[:, :width], jnp.full((EXTRA, width), EMPTY, BF16)], axis=0)
    picked = dot(pick, rows, 0, 0).astype(BF16)
    out_ref[...] = picked.reshape(out_ref.shape)


def parts_kernel(rows_ref, gate_ref, up_ref, down_ref, main_ref, rest_ref, place_ref, count_ref):
    parts, main, _ = main_ref.shape
    slots = rows_ref.shape[0]
    width = gate_ref.shape[0]
    named = rows_ref[:, :LANES].astype(F32)[:, :1] < 0.5 * EMPTY
    named_wide = jnp.broadcast_to(named.astype(F32), (slots, LANES))
    before = (iota((slots, slots), 1) < iota((slots, slots), 0)).astype(BF16)
    order = dot(before, named_wide.astype(BF16))[:, :1].astype(jnp.int32)
    place = (jnp.where(named, order, slots) == iota((slots, slots), 1)).astype(BF16)
    place_ref[...] = place
    count_ref[0, 0] = jnp.sum(named_wide[:, :1]).astype(jnp.int32)
    x = dot(place, rows_ref[:, :width], 0, 0).astype(BF16)
    y = dot(place, rows_ref[:, width:], 0, 0).astype(BF16)
    for j in range(0, parts, 2):
        step = min(2, parts - j)
        cols = slice(j * LANES, (j + step) * LANES)
        products = (
            dot(x, gate_ref[:, cols]),
            dot(x, up_ref[:, cols]),
            dot(y, down_ref[cols, :], 1, 1),
        )
        for i in range(step):
            for at, value in enumerate(products):
                piece = value[:, i * LANES : (i + 1) * LANES].astype(BF16)
                main_ref[j + i, :, at * LANES : (at + 1) * LANES] = piece[:main]
                rest_ref[j + i, :, at * LANES : (at + 1) * LANES] = piece[main:]


def hidden_kernel(parts_ref, out_ref):
    parts, rows, _ = parts_ref.shape
    total = parts_ref[0].astype(F32)
    for j in range(1, parts):
        total += parts_ref[j].astype(F32)
    gate_pre = total[:, :LANES]
    up_pre = total[:, LANES : 2 * LANES]
    grad_act = total[:, 2 * LANES :]
    sig = jax.nn.sigmoid(gate_pre)
    silu_val = gate_pre * sig
    product = silu_val * up_pre * grad_act
    grad_gate = (grad_act * up_pre * sig * (1.0 + gate_pre * (1.0 - sig))).astype(BF16)
    grad_up = (grad_act * silu_val).astype(BF16)
    score = lax.dot_general(
        jnp.ones((8, LANES), F32), product, (((1,), (1,)), ((), ())),
        preferred_element_type=F32, precision=lax.Precision.HIGHEST,
    )
    high = score.astype(BF16).astype(F32)
    tail = jnp.concatenate([high, score - high], axis=0).astype(BF16)
    pad = jnp.zeros((EXTRA, 2 * LANES - rows), BF16) if rows < 2 * LANES else None
    if pad is not None:
        tail = jnp.concatenate([tail, pad], axis=1)
    for j in range(parts):
        out_ref[j, :rows, :LANES] = grad_gate
        out_ref[j, :rows, LANES:] = grad_up
        out_ref[j, rows:, :] = tail


def back_rows(hidden_ref, gate_ref, up_ref):
    parts, rows, _ = hidden_ref.shape
    rows -= EXTRA
    width = gate_ref.shape[0]
    total = jnp.zeros((rows, width), F32)
    score = jnp.zeros((8, 2 * LANES), F32)
    for j in range(parts):
        cols = slice(j * LANES, (j + 1) * LANES)
        weights = jnp.concatenate([gate_ref[:, cols], up_ref[:, cols]], axis=1)
        total += dot(hidden_ref[j, :rows, :], weights, 1, 1)
        tail = hidden_ref[j, rows:, :].astype(F32)
        score += tail[:8] + tail[8:]
    score = score.astype(BF16)
    unit = (iota((rows, 2 * LANES), 0) == iota((rows, 2 * LANES), 1)).astype(BF16)
    spread = jnp.concatenate([score] * (LANES // 8), axis=0)
    return total.astype(BF16), dot(unit, spread, 1, 1).astype(BF16)


def rest_kernel(hidden_ref, gate_ref, up_ref, out_ref):
    width = gate_ref.shape[0]
    out_ref[:, :width], out_ref[:, width:] = back_rows(hidden_ref, gate_ref, up_ref)


def back_kernel(hidden_ref, gate_ref, up_ref, rest_ref, place_ref, out_ref):
    width = gate_ref.shape[0]
    main, main_score = back_rows(hidden_ref, gate_ref, up_ref)
    rows = jnp.concatenate([main, rest_ref[:, :width]], axis=0)
    out_ref[:, :width] = dot(place_ref[...], rows).astype(BF16)
    score = jnp.concatenate([main_score, rest_ref[:, width:]], axis=0)
    out_ref[:, width:] = dot(place_ref[...], score).astype(BF16)


def combine_kernel(routes, slot_cap, tok_ref, back_ref, out_ref):
    groups, toks, full = tok_ref.shape
    size = back_ref.shape[0]
    width = back_ref.shape[2] - LANES
    facts = tok_ref[:, :, full - LANES :].reshape(groups * toks, LANES).astype(F32)
    back = back_ref[...].reshape(size * groups * slot_cap, width + LANES)
    hits, _ = route_hits(facts, groups, toks, size, slot_cap, routes)
    weight = jnp.zeros(hits[0].shape, F32)
    for k in range(routes):
        value = sum(facts[:, i * routes + k : i * routes + k + 1] for i in (1, 2, 3))
        weight = jnp.where(hits[k], value, weight)
    sums = sum(dot(piece, back[:, :width]) for piece in split_three(weight))
    lane = iota((groups * toks, LANES), 1)
    scores = jnp.zeros((groups * toks, LANES), F32)
    for k in range(routes):
        scores = jnp.where(lane == k, dot(hits[k].astype(BF16), back[:, width:]), scores)
    out_ref[:, :, :width] = sums.astype(BF16).reshape(groups, toks, width)
    out_ref[:, :, width:] = scores.astype(BF16).reshape(groups, toks, LANES)


def home_kernel(parts_ref, grad_ref, score_ref):
    groups, toks, _ = parts_ref.shape
    width = grad_ref.shape[1]
    total = parts_ref[0].astype(F32)
    for group in range(1, groups):
        total += parts_ref[group].astype(F32)
    grad_ref[...] = total[:, :width].astype(BF16)
    unit = (iota((toks, toks), 0) == iota((toks, toks), 1)).astype(BF16)
    scores = dot(total[:, width:].astype(BF16), unit, 0, 0)
    score_ref[...] = scores[: score_ref.shape[0]].astype(BF16)


def on_device(hidden_in, grad_out, expert_ids, route_weights, gate_weight, up_weight, down_weight):
    node_count = lax.axis_size("node")
    parts = lax.axis_size("local")
    tok_count, width = hidden_in.shape
    group_count = min(8, node_count // 2)
    group_size = node_count // group_count
    slot_cap = 2 * tok_count // group_size
    slot_total = node_count * slot_cap
    routes = expert_ids.shape[1]
    across = [[g * group_size + p for g in range(group_count)] for p in range(group_size)]
    within = [[g * group_size + p for p in range(group_size)] for g in range(group_count)]

    def swap(value, axis, members=None):
        return lax.all_to_all(
            value, axis, split_axis=0, concat_axis=0, tiled=True, axis_index_groups=members
        )

    w_gate, w_up, w_down = gate_weight[0], up_weight[0], down_weight[0]

    def call(kernel, shape, *args):
        return pl.pallas_call(
            kernel,
            out_shape=jax.tree.map(lambda s: jax.ShapeDtypeStruct(s, BF16), shape, is_leaf=lambda s: isinstance(s, tuple) and isinstance(s[0], int)),
            compiler_params=PARAMS,
        )(*args)

    own = (expert_ids.T, route_weights.T, hidden_in, grad_out)
    tokens = pl.pallas_call(
        functools.partial(pack_kernel, group_size),
        out_shape=jax.ShapeDtypeStruct((group_count, tok_count, 2 * width + LANES), BF16),
        in_specs=[pl.BlockSpec(memory_space=pltpu.HBM)] * len(own),
        scratch_shapes=[pltpu.VMEM(value.shape, value.dtype) for value in own]
        + [pltpu.SemaphoreType.DMA((len(own),))],
        compiler_params=pltpu.CompilerParams(vmem_limit_bytes=56 * 1024 * 1024),
    )(*own)
    tokens = swap(tokens, "node", across)
    rows = call(
        functools.partial(rows_kernel, routes, slot_cap),
        (group_size, group_count * slot_cap, 2 * width), tokens,
    )
    rows = swap(rows, "node", within).reshape(slot_total, 2 * width)
    main = max(EXTRA, slot_total * 5 // 8 // EXTRA * EXTRA)
    vmem = pl.BlockSpec(memory_space=pltpu.VMEM)
    main_sums, rest_sums, place, count = pl.pallas_call(
        parts_kernel,
        out_shape=[
            jax.ShapeDtypeStruct((parts, main, 3 * LANES), BF16),
            jax.ShapeDtypeStruct((parts, slot_total - main, 3 * LANES), BF16),
            jax.ShapeDtypeStruct((slot_total, slot_total), BF16),
            jax.ShapeDtypeStruct((1, 1), jnp.int32),
        ],
        out_specs=[vmem, vmem, vmem, pl.BlockSpec(memory_space=pltpu.SMEM)],
        compiler_params=PARAMS,
    )(rows, w_gate, w_up, w_down)

    def over_local(sums):
        sums = swap(sums, "local")
        hidden = call(hidden_kernel, (parts, sums.shape[1] + EXTRA, 2 * LANES), sums)
        return swap(hidden, "local")

    def rest_of(sums, w_gate, w_up):
        return call(rest_kernel, (slot_total - main, width + LANES), over_local(sums), w_gate, w_up)

    rest = lax.cond(
        count[0, 0] > main,
        rest_of,
        lambda *_: jnp.zeros((slot_total - main, width + LANES), BF16),
        rest_sums, w_gate, w_up,
    )
    hidden = over_local(main_sums)
    back = call(back_kernel, (slot_total, width + LANES), hidden, w_gate, w_up, rest, place)
    back = swap(back.reshape(group_size, group_count * slot_cap, width + LANES), "node", within)
    home = call(
        functools.partial(combine_kernel, routes, slot_cap),
        (group_count, tok_count, width + LANES), tokens, back,
    )
    home = swap(home, "node", across)
    grad_in, scores = call(home_kernel, [(tok_count, width), (routes, tok_count)], home)
    return (grad_in, scores.T)


def solution(mesh):
    return jax.shard_map(
        on_device,
        mesh=mesh,
        in_specs=(
            P("node", "local"),
            P("node", "local"),
            P("node", None),
            P("node", None),
            P("node", "local", None),
            P("node", "local", None),
            P("node", None, "local"),
        ),
        out_specs=(P("node", "local"), P("node", None)),
        check_vma=False,
    )
```

```python
import functools

import jax
import jax.numpy as jnp
from jax import lax
from jax.experimental import pallas as pl
from jax.experimental.pallas import tpu as pltpu
from jax.sharding import PartitionSpec as P

BF16 = jnp.bfloat16
F32 = jnp.float32
EMPTY = 64.0
LANES = 128
EXTRA = 16
PARAMS = pltpu.CompilerParams(vmem_limit_bytes=32 * 1024 * 1024)


def dot(left, right, left_dim=1, right_dim=0):
    return lax.dot_general(
        left, right, (((left_dim,), (right_dim,)), ((), ())), preferred_element_type=F32
    )


def iota(shape, dim):
    return lax.broadcasted_iota(jnp.int32, shape, dim)


def split_three(value):
    high = value.astype(BF16)
    rest = value - high.astype(F32)
    middle = rest.astype(BF16)
    return high, middle, (rest - middle.astype(F32)).astype(BF16)


def pack_kernel(size, ids_in, route_in, x_in, y_in, out_ref, ids_ref, route_ref, x_ref, y_ref, sems):
    pairs = ((ids_in, ids_ref), (route_in, route_ref), (x_in, x_ref), (y_in, y_ref))
    copies = [pltpu.make_async_copy(*pair, sems.at[i]) for i, pair in enumerate(pairs)]
    for copy in copies:
        copy.start()
    for copy in copies:
        copy.wait()
    groups, toks, _ = out_ref.shape
    routes = ids_ref.shape[0]
    width = x_ref.shape[1]
    unit = (iota((toks, toks), 0) == iota((toks, toks), 1)).astype(BF16)
    pieces = [piece.astype(F32) for piece in split_three(route_ref[...])]
    fill = jnp.zeros((LANES - 4 * routes, toks), F32)
    for group in range(groups):
        ids = (ids_ref[...] - group * size).astype(F32)
        facts = jnp.concatenate([ids, *pieces, fill], axis=0).astype(BF16)
        out_ref[group, :, :width] = x_ref[...]
        out_ref[group, :, width : 2 * width] = y_ref[...]
        out_ref[group, :, 2 * width :] = dot(unit, facts, 1, 1).astype(BF16)


def route_hits(facts, groups, toks, size, slot_cap, routes):
    shape = (groups * toks, size * groups * slot_cap)
    column = iota(shape, 1)
    expert = column // (groups * slot_cap)
    names = [facts[:, k : k + 1].astype(jnp.int32) == expert for k in range(routes)]
    named = functools.reduce(jnp.logical_or, names)
    square = (groups * toks, groups * toks)
    one, two = iota(square, 0), iota(square, 1)
    before = ((one // toks == two // toks) & (two < one)).astype(BF16)
    earlier = dot(before, named.astype(BF16)).astype(jnp.int32)
    here = (earlier == column % slot_cap) & (
        column // slot_cap % groups == iota(shape, 0) // toks
    )
    return [name & here for name in names], named & here


def rows_kernel(routes, slot_cap, tok_ref, out_ref):
    groups, toks, full = tok_ref.shape
    size = out_ref.shape[0]
    width = full - LANES
    toks_all = tok_ref[...].reshape(groups * toks, full)
    facts = toks_all[:, width:].astype(F32)
    _, taken = route_hits(facts, groups, toks, size, slot_cap, routes)
    taken = taken.astype(F32)
    free = 1.0 - jnp.sum(taken, axis=0, keepdims=True)
    shape = (EXTRA, taken.shape[1])
    free = jnp.where(iota(shape, 0) == 0, jnp.broadcast_to(free, shape), 0.0)
    pick = jnp.concatenate([taken, free], axis=0).astype(BF16)
    rows = jnp.concatenate([toks_all[:, :width], jnp.full((EXTRA, width), EMPTY, BF16)], axis=0)
    picked = dot(pick, rows, 0, 0).astype(BF16)
    out_ref[...] = picked.reshape(out_ref.shape)


def products(x, y, gate_ref, up_ref, down_ref, out_ref):
    parts = out_ref.shape[0]
    for j in range(0, parts, 2):
        step = min(2, parts - j)
        cols = slice(j * LANES, (j + step) * LANES)
        values = (
            dot(x, gate_ref[:, cols]),
            dot(y, down_ref[cols, :], 1, 1),
            dot(x, up_ref[:, cols]),
        )
        for i in range(step):
            for at, value in zip((0, 2, 1), values):
                out_ref[j + i, :, at * LANES : (at + 1) * LANES] = value[
                    :, i * LANES : (i + 1) * LANES
                ].astype(BF16)


def parts_kernel(
    rows_ref, gate_ref, up_in, down_ref, main_ref, rest_out, place_ref, count_ref, up_ref, rest_ref, sems
):
    up_copy = pltpu.make_async_copy(up_in, up_ref, sems.at[0])
    up_copy.start()
    main = main_ref.shape[1]
    slots = rows_ref.shape[0]
    width = gate_ref.shape[0]
    named = rows_ref[:, :LANES].astype(F32)[:, :1] < 0.5 * EMPTY
    named_wide = jnp.broadcast_to(named.astype(F32), (slots, LANES))
    count = jnp.sum(named_wide[:, :1]).astype(jnp.int32)
    count_ref[0, 0] = count
    before = (iota((slots, slots), 1) < iota((slots, slots), 0)).astype(BF16)
    order = dot(before, named_wide.astype(BF16))[:, :1].astype(jnp.int32)
    place = (jnp.where(named, order, slots) == iota((slots, slots), 1)).astype(BF16)
    place_ref[...] = place
    x = dot(place[:, :main], rows_ref[:, :width], 0, 0).astype(BF16)
    y = dot(place[:, :main], rows_ref[:, width:], 0, 0).astype(BF16)
    up_copy.wait()
    products(x, y, gate_ref, up_ref, down_ref, main_ref)

    @pl.when(count > main)
    def _():
        last = place_ref[:, main:]
        x = dot(last, rows_ref[:, :width], 0, 0).astype(BF16)
        y = dot(last, rows_ref[:, width:], 0, 0).astype(BF16)
        products(x, y, gate_ref, up_ref, down_ref, rest_ref)
        rest_copy = pltpu.make_async_copy(rest_ref, rest_out, sems.at[1])
        rest_copy.start()
        rest_copy.wait()


def hidden_kernel(parts_ref, out_ref):
    parts, rows, _ = parts_ref.shape
    total = parts_ref[0].astype(F32)
    for j in range(1, parts):
        total += parts_ref[j].astype(F32)
    gate_pre = total[:, :LANES]
    up_pre = total[:, LANES : 2 * LANES]
    grad_act = total[:, 2 * LANES :]
    sig = jax.nn.sigmoid(gate_pre)
    silu_val = gate_pre * sig
    product = silu_val * up_pre * grad_act
    grad_gate = (grad_act * up_pre * sig * (1.0 + gate_pre * (1.0 - sig))).astype(BF16)
    grad_up = (grad_act * silu_val).astype(BF16)
    score = lax.dot_general(
        jnp.ones((8, LANES), F32), product, (((1,), (1,)), ((), ())),
        preferred_element_type=F32, precision=lax.Precision.HIGHEST,
    )
    high = score.astype(BF16).astype(F32)
    tail = jnp.concatenate([high, score - high], axis=0).astype(BF16)
    pad = jnp.zeros((EXTRA, 2 * LANES - rows), BF16) if rows < 2 * LANES else None
    if pad is not None:
        tail = jnp.concatenate([tail, pad], axis=1)
    for j in range(parts):
        out_ref[j, :rows, :LANES] = grad_gate
        out_ref[j, :rows, LANES:] = grad_up
        out_ref[j, rows:, :] = tail


def back_rows(hidden_ref, gate_ref, up_ref):
    parts, rows, _ = hidden_ref.shape
    rows -= EXTRA
    width = gate_ref.shape[0]
    total = jnp.zeros((rows, width), F32)
    score = jnp.zeros((8, 2 * LANES), F32)
    for j in range(parts):
        cols = slice(j * LANES, (j + 1) * LANES)
        weights = jnp.concatenate([gate_ref[:, cols], up_ref[:, cols]], axis=1)
        total += dot(hidden_ref[j, :rows, :], weights, 1, 1)
        tail = hidden_ref[j, rows:, :].astype(F32)
        score += tail[:8] + tail[8:]
    score = score.astype(BF16)
    unit = (iota((rows, 2 * LANES), 0) == iota((rows, 2 * LANES), 1)).astype(BF16)
    spread = jnp.concatenate([score] * (LANES // 8), axis=0)
    return total.astype(BF16), dot(unit, spread, 1, 1).astype(BF16)


def back_kernel(hidden_ref, gate_ref, up_ref, place_ref, count_ref, out_ref, count_out):
    count_out[0, 0] = count_ref[0, 0]
    width = gate_ref.shape[0]
    rows, score = back_rows(hidden_ref, gate_ref, up_ref)
    place = place_ref[:, : rows.shape[0]]
    out_ref[:, :width] = dot(place, rows).astype(BF16)
    out_ref[:, width:] = dot(place, score).astype(BF16)


def rest_kernel(hidden_ref, gate_ref, up_ref, place_ref, main_ref, out_ref):
    width = gate_ref.shape[0]
    rows, score = back_rows(hidden_ref, gate_ref, up_ref)
    place = place_ref[:, place_ref.shape[1] - rows.shape[0] :]
    out_ref[:, :width] = (main_ref[:, :width].astype(F32) + dot(place, rows)).astype(BF16)
    out_ref[:, width:] = (main_ref[:, width:].astype(F32) + dot(place, score)).astype(BF16)


def combine_kernel(routes, slot_cap, tok_ref, back_ref, out_ref):
    groups, toks, full = tok_ref.shape
    size = back_ref.shape[0]
    width = back_ref.shape[2] - LANES
    facts = tok_ref[:, :, full - LANES :].reshape(groups * toks, LANES).astype(F32)
    back = back_ref[...].reshape(size * groups * slot_cap, width + LANES)
    hits, _ = route_hits(facts, groups, toks, size, slot_cap, routes)
    weight = jnp.zeros(hits[0].shape, F32)
    for k in range(routes):
        value = sum(facts[:, i * routes + k : i * routes + k + 1] for i in (1, 2, 3))
        weight = jnp.where(hits[k], value, weight)
    sums = sum(dot(piece, back[:, :width]) for piece in split_three(weight))
    lane = iota((groups * toks, LANES), 1)
    scores = jnp.zeros((groups * toks, LANES), F32)
    for k in range(routes):
        scores = jnp.where(lane == k, dot(hits[k].astype(BF16), back[:, width:]), scores)
    out_ref[:, :, :width] = sums.astype(BF16).reshape(groups, toks, width)
    out_ref[:, :, width:] = scores.astype(BF16).reshape(groups, toks, LANES)


def home_kernel(parts_ref, grad_ref, score_ref):
    groups, toks, _ = parts_ref.shape
    width = grad_ref.shape[1]
    total = parts_ref[0].astype(F32)
    for group in range(1, groups):
        total += parts_ref[group].astype(F32)
    grad_ref[...] = total[:, :width].astype(BF16)
    unit = (iota((toks, toks), 0) == iota((toks, toks), 1)).astype(BF16)
    scores = dot(total[:, width:].astype(BF16), unit, 0, 0)
    score_ref[...] = scores[: score_ref.shape[0]].astype(BF16)


def on_device(hidden_in, grad_out, expert_ids, route_weights, gate_weight, up_weight, down_weight):
    node_count = lax.axis_size("node")
    parts = lax.axis_size("local")
    tok_count, width = hidden_in.shape
    group_count = min(8, node_count // 2)
    group_size = node_count // group_count
    slot_cap = 2 * tok_count // group_size
    slot_total = node_count * slot_cap
    routes = expert_ids.shape[1]
    across = [[g * group_size + p for g in range(group_count)] for p in range(group_size)]
    within = [[g * group_size + p for p in range(group_size)] for g in range(group_count)]

    vmem = pl.BlockSpec(memory_space=pltpu.VMEM)
    smem = pl.BlockSpec(memory_space=pltpu.SMEM)
    hbm = pl.BlockSpec(memory_space=pltpu.HBM)

    def swap(value, axis, members=None):
        return lax.all_to_all(
            value, axis, split_axis=0, concat_axis=0, tiled=True, axis_index_groups=members
        )

    w_gate, w_up, w_down = gate_weight[0], up_weight[0], down_weight[0]

    def call(kernel, shape, *args):
        return pl.pallas_call(
            kernel,
            out_shape=jax.tree.map(lambda s: jax.ShapeDtypeStruct(s, BF16), shape, is_leaf=lambda s: isinstance(s, tuple) and isinstance(s[0], int)),
            compiler_params=PARAMS,
        )(*args)

    own = (expert_ids.T, route_weights.T, hidden_in, grad_out)
    tokens = pl.pallas_call(
        functools.partial(pack_kernel, group_size),
        out_shape=jax.ShapeDtypeStruct((group_count, tok_count, 2 * width + LANES), BF16),
        in_specs=[hbm] * len(own),
        scratch_shapes=[pltpu.VMEM(value.shape, value.dtype) for value in own]
        + [pltpu.SemaphoreType.DMA((len(own),))],
        compiler_params=pltpu.CompilerParams(vmem_limit_bytes=56 * 1024 * 1024),
    )(*own)
    tokens = swap(tokens, "node", across)
    rows = call(
        functools.partial(rows_kernel, routes, slot_cap),
        (group_size, group_count * slot_cap, 2 * width), tokens,
    )
    rows = swap(rows, "node", within).reshape(slot_total, 2 * width)
    main = max(EXTRA, slot_total * 5 // 8 // EXTRA * EXTRA)
    rest_shape = (parts, slot_total - main, 3 * LANES)
    main_sums, rest_sums, place, count = pl.pallas_call(
        parts_kernel,
        out_shape=[
            jax.ShapeDtypeStruct((parts, main, 3 * LANES), BF16),
            jax.ShapeDtypeStruct(rest_shape, BF16),
            jax.ShapeDtypeStruct((slot_total, slot_total), BF16),
            jax.ShapeDtypeStruct((1, 1), jnp.int32),
        ],
        in_specs=[vmem, vmem, hbm, vmem],
        out_specs=[vmem, hbm, vmem, smem],
        scratch_shapes=[
            pltpu.VMEM(w_up.shape, BF16),
            pltpu.VMEM(rest_shape, BF16),
            pltpu.SemaphoreType.DMA((2,)),
        ],
        compiler_params=PARAMS,
    )(rows, w_gate, w_up, w_down)

    def over_local(sums):
        sums = swap(sums, "local")
        hidden = call(hidden_kernel, (parts, sums.shape[1] + EXTRA, 2 * LANES), sums)
        return swap(hidden, "local")

    hidden = over_local(main_sums)
    back, count = pl.pallas_call(
        back_kernel,
        out_shape=[
            jax.ShapeDtypeStruct((slot_total, width + LANES), BF16),
            jax.ShapeDtypeStruct((1, 1), jnp.int32),
        ],
        in_specs=[vmem, vmem, vmem, vmem, smem],
        out_specs=[vmem, smem],
        compiler_params=PARAMS,
    )(hidden, w_gate, w_up, place, count)

    def add_rest(back, sums, place, w_gate, w_up):
        return call(rest_kernel, (slot_total, width + LANES), over_local(sums), w_gate, w_up, place, back)

    back = lax.cond(
        count[0, 0] > main, add_rest, lambda back, *_: back, back, rest_sums, place, w_gate, w_up
    )
    back = swap(back.reshape(group_size, group_count * slot_cap, width + LANES), "node", within)
    home = call(
        functools.partial(combine_kernel, routes, slot_cap),
        (group_count, tok_count, width + LANES), tokens, back,
    )
    home = swap(home, "node", across)
    grad_in, scores = call(home_kernel, [(tok_count, width), (routes, tok_count)], home)
    return (grad_in, scores.T)


def solution(mesh):
    return jax.shard_map(
        on_device,
        mesh=mesh,
        in_specs=(
            P("node", "local"),
            P("node", "local"),
            P("node", None),
            P("node", None),
            P("node", "local", None),
            P("node", "local", None),
            P("node", None, "local"),
        ),
        out_specs=(P("node", "local"), P("node", None)),
        check_vma=False,
    )
```

```python
import functools

import jax
import jax.numpy as jnp
from jax import lax
from jax.experimental import pallas as pl
from jax.experimental.pallas import tpu as pltpu
from jax.sharding import PartitionSpec as P

BF16 = jnp.bfloat16
F32 = jnp.float32
EMPTY = 64.0
LANES = 128
EXTRA = 16
TAIL = 8
PARAMS = pltpu.CompilerParams(vmem_limit_bytes=32 * 1024 * 1024)


def dot(left, right, left_dim=1, right_dim=0):
    return lax.dot_general(
        left, right, (((left_dim,), (right_dim,)), ((), ())), preferred_element_type=F32
    )


def iota(shape, dim):
    return lax.broadcasted_iota(jnp.int32, shape, dim)


def split_three(value):
    high = value.astype(BF16)
    rest = value - high.astype(F32)
    middle = rest.astype(BF16)
    return high, middle, (rest - middle.astype(F32)).astype(BF16)


def pack_kernel(size, ids_in, route_in, x_in, y_in, out_ref, ids_ref, route_ref, x_ref, y_ref, sems):
    pairs = ((ids_in, ids_ref), (route_in, route_ref), (x_in, x_ref), (y_in, y_ref))
    copies = [pltpu.make_async_copy(*pair, sems.at[i]) for i, pair in enumerate(pairs)]
    for copy in copies:
        copy.start()
    for copy in copies:
        copy.wait()
    groups, toks, _ = out_ref.shape
    routes = ids_ref.shape[0]
    width = x_ref.shape[1]
    unit = (iota((toks, toks), 0) == iota((toks, toks), 1)).astype(BF16)
    pieces = [piece.astype(F32) for piece in split_three(route_ref[...])]
    fill = jnp.zeros((LANES - 4 * routes, toks), F32)
    for group in range(groups):
        ids = (ids_ref[...] - group * size).astype(F32)
        facts = jnp.concatenate([ids, *pieces, fill], axis=0).astype(BF16)
        out_ref[group, :, :width] = x_ref[...]
        out_ref[group, :, width : 2 * width] = y_ref[...]
        out_ref[group, :, 2 * width :] = dot(unit, facts, 1, 1).astype(BF16)


def route_hits(facts, groups, toks, size, slot_cap, routes):
    shape = (groups * toks, size * groups * slot_cap)
    column = iota(shape, 1)
    expert = column // (groups * slot_cap)
    names = [facts[:, k : k + 1].astype(jnp.int32) == expert for k in range(routes)]
    named = functools.reduce(jnp.logical_or, names)
    square = (groups * toks, groups * toks)
    one, two = iota(square, 0), iota(square, 1)
    before = ((one // toks == two // toks) & (two < one)).astype(BF16)
    earlier = dot(before, named.astype(BF16)).astype(jnp.int32)
    here = (earlier == column % slot_cap) & (
        column // slot_cap % groups == iota(shape, 0) // toks
    )
    return [name & here for name in names], named & here


def rows_kernel(routes, slot_cap, tok_ref, out_ref):
    groups, toks, full = tok_ref.shape
    size = out_ref.shape[0]
    width = full - LANES
    toks_all = tok_ref[...].reshape(groups * toks, full)
    facts = toks_all[:, width:].astype(F32)
    _, taken = route_hits(facts, groups, toks, size, slot_cap, routes)
    taken = taken.astype(F32)
    free = 1.0 - jnp.sum(taken, axis=0, keepdims=True)
    shape = (EXTRA, taken.shape[1])
    free = jnp.where(iota(shape, 0) == 0, jnp.broadcast_to(free, shape), 0.0)
    pick = jnp.concatenate([taken, free], axis=0).astype(BF16)
    rows = jnp.concatenate([toks_all[:, :width], jnp.full((EXTRA, width), EMPTY, BF16)], axis=0)
    picked = dot(pick, rows, 0, 0).astype(BF16)
    out_ref[...] = picked.reshape(out_ref.shape)


def products(x, y, gate_ref, up_ref, down_ref, out_ref):
    parts = out_ref.shape[0]
    for j in range(0, parts, 2):
        step = min(2, parts - j)
        cols = slice(j * LANES, (j + step) * LANES)
        values = (
            dot(x, gate_ref[:, cols]),
            dot(y, down_ref[cols, :], 1, 1),
            dot(x, up_ref[:, cols]),
        )
        for i in range(step):
            for at, value in zip((0, 2, 1), values):
                out_ref[j + i, :, at * LANES : (at + 1) * LANES] = value[
                    :, i * LANES : (i + 1) * LANES
                ].astype(BF16)


def parts_kernel(
    rows_ref, gate_ref, up_in, down_ref, main_ref, rest_out, place_ref, count_ref, up_ref, rest_ref, sems
):
    up_copy = pltpu.make_async_copy(up_in, up_ref, sems.at[0])
    up_copy.start()
    main = main_ref.shape[1]
    slots = rows_ref.shape[0]
    width = gate_ref.shape[0]
    named = rows_ref[:, :LANES].astype(F32)[:, :1] < 0.5 * EMPTY
    named_wide = jnp.broadcast_to(named.astype(F32), (slots, LANES))
    count = jnp.sum(named_wide[:, :1]).astype(jnp.int32)
    count_ref[0, 0] = count
    before = (iota((slots, slots), 1) < iota((slots, slots), 0)).astype(BF16)
    order = dot(before, named_wide.astype(BF16))[:, :1].astype(jnp.int32)
    place = (jnp.where(named, order, slots) == iota((slots, slots), 1)).astype(BF16)
    place_ref[...] = place
    packed = dot(place, rows_ref[...], 0, 0).astype(BF16)
    x, y = packed[:main, :width], packed[:main, width:]
    up_copy.wait()
    products(x, y, gate_ref, up_ref, down_ref, main_ref)

    @pl.when(count > main)
    def _():
        packed = dot(place_ref[...], rows_ref[...], 0, 0).astype(BF16)
        x, y = packed[main:, :width], packed[main:, width:]
        products(x, y, gate_ref, up_ref, down_ref, rest_ref)
        rest_copy = pltpu.make_async_copy(rest_ref, rest_out, sems.at[1])
        rest_copy.start()
        rest_copy.wait()


def hidden_kernel(parts_ref, out_ref):
    parts, rows, _ = parts_ref.shape
    total = parts_ref[0].astype(F32)
    for j in range(1, parts):
        total += parts_ref[j].astype(F32)
    gate_pre = total[:, :LANES]
    up_pre = total[:, LANES : 2 * LANES]
    grad_act = total[:, 2 * LANES :]
    sig = jax.nn.sigmoid(gate_pre)
    silu_val = gate_pre * sig
    product = silu_val * up_pre * grad_act
    grad_gate = (grad_act * up_pre * sig * (1.0 + gate_pre * (1.0 - sig))).astype(BF16)
    grad_up = (grad_act * silu_val).astype(BF16)
    score = lax.dot_general(
        jnp.ones((8, LANES), F32), product, (((1,), (1,)), ((), ())),
        preferred_element_type=F32, precision=lax.Precision.HIGHEST,
    )
    high = score.astype(BF16).astype(F32)
    tail = jnp.where(iota(score.shape, 0) < 4, high, score - high).astype(BF16)
    pad = jnp.zeros((TAIL, 2 * LANES - rows), BF16) if rows < 2 * LANES else None
    if pad is not None:
        tail = jnp.concatenate([tail, pad], axis=1)
    for j in range(parts):
        out_ref[j, :rows, :LANES] = grad_gate
        out_ref[j, :rows, LANES:] = grad_up
        out_ref[j, rows:, :] = tail


def back_rows(hidden_ref, gate_ref, up_ref):
    parts, rows, _ = hidden_ref.shape
    rows -= TAIL
    width = gate_ref.shape[0]
    total = jnp.zeros((rows, width), F32)
    tails = jnp.zeros((TAIL, 2 * LANES), F32)
    for j in range(parts):
        cols = slice(j * LANES, (j + 1) * LANES)
        weights = jnp.concatenate([gate_ref[:, cols], up_ref[:, cols]], axis=1)
        total += dot(hidden_ref[j, :rows, :], weights, 1, 1)
        tails += hidden_ref[j, rows:, :].astype(F32)
    score = jnp.broadcast_to(tails[:1] + tails[4:5], tails.shape).astype(BF16)
    unit = (iota((rows, 2 * LANES), 0) == iota((rows, 2 * LANES), 1)).astype(BF16)
    spread = jnp.concatenate([score] * (LANES // 8), axis=0)
    return total.astype(BF16), dot(unit, spread, 1, 1).astype(BF16)


def back_kernel(hidden_ref, gate_ref, up_ref, place_ref, count_ref, out_ref, count_out):
    count_out[0, 0] = count_ref[0, 0]
    rows = jnp.concatenate(back_rows(hidden_ref, gate_ref, up_ref), axis=1)
    fill = jnp.zeros((place_ref.shape[1] - rows.shape[0], rows.shape[1]), BF16)
    out_ref[...] = dot(place_ref[...], jnp.concatenate([rows, fill], axis=0)).astype(BF16)


def rest_kernel(hidden_ref, gate_ref, up_ref, place_ref, main_ref, out_ref):
    width = gate_ref.shape[0]
    rows, score = back_rows(hidden_ref, gate_ref, up_ref)
    place = place_ref[:, place_ref.shape[1] - rows.shape[0] :]
    out_ref[:, :width] = (main_ref[:, :width].astype(F32) + dot(place, rows)).astype(BF16)
    out_ref[:, width:] = (main_ref[:, width:].astype(F32) + dot(place, score)).astype(BF16)


def combine_kernel(routes, slot_cap, tok_ref, back_ref, out_ref):
    groups, toks, full = tok_ref.shape
    size = back_ref.shape[0]
    width = back_ref.shape[2] - LANES
    facts = tok_ref[:, :, full - LANES :].reshape(groups * toks, LANES).astype(F32)
    back = back_ref[...].reshape(size * groups * slot_cap, width + LANES)
    hits, _ = route_hits(facts, groups, toks, size, slot_cap, routes)
    weight = jnp.zeros(hits[0].shape, F32)
    for k in range(routes):
        value = sum(facts[:, i * routes + k : i * routes + k + 1] for i in (1, 2, 3))
        weight = jnp.where(hits[k], value, weight)
    sums = sum(dot(piece, back[:, :width]) for piece in split_three(weight))
    lane = iota((groups * toks, LANES), 1)
    scores = jnp.zeros((groups * toks, LANES), F32)
    for k in range(routes):
        scores = jnp.where(lane == k, dot(hits[k].astype(BF16), back[:, width:]), scores)
    out_ref[:, :, :width] = sums.astype(BF16).reshape(groups, toks, width)
    out_ref[:, :, width:] = scores.astype(BF16).reshape(groups, toks, LANES)


def home_kernel(parts_ref, grad_ref, score_ref):
    groups, toks, _ = parts_ref.shape
    width = grad_ref.shape[1]
    total = parts_ref[0].astype(F32)
    for group in range(1, groups):
        total += parts_ref[group].astype(F32)
    grad_ref[...] = total[:, :width].astype(BF16)
    unit = (iota((toks, toks), 0) == iota((toks, toks), 1)).astype(BF16)
    scores = dot(total[:, width:].astype(BF16), unit, 0, 0)
    score_ref[...] = scores[: score_ref.shape[0]].astype(BF16)


def on_device(hidden_in, grad_out, expert_ids, route_weights, gate_weight, up_weight, down_weight):
    node_count = lax.axis_size("node")
    parts = lax.axis_size("local")
    tok_count, width = hidden_in.shape
    group_count = min(8, node_count // 2)
    group_size = node_count // group_count
    slot_cap = 2 * tok_count // group_size
    slot_total = node_count * slot_cap
    routes = expert_ids.shape[1]
    across = [[g * group_size + p for g in range(group_count)] for p in range(group_size)]
    within = [[g * group_size + p for p in range(group_size)] for g in range(group_count)]

    vmem = pl.BlockSpec(memory_space=pltpu.VMEM)
    smem = pl.BlockSpec(memory_space=pltpu.SMEM)
    hbm = pl.BlockSpec(memory_space=pltpu.HBM)

    def swap(value, axis, members=None):
        return lax.all_to_all(
            value, axis, split_axis=0, concat_axis=0, tiled=True, axis_index_groups=members
        )

    w_gate, w_up, w_down = gate_weight[0], up_weight[0], down_weight[0]

    def call(kernel, shape, *args):
        return pl.pallas_call(
            kernel,
            out_shape=jax.tree.map(lambda s: jax.ShapeDtypeStruct(s, BF16), shape, is_leaf=lambda s: isinstance(s, tuple) and isinstance(s[0], int)),
            compiler_params=PARAMS,
        )(*args)

    own = (expert_ids.T, route_weights.T, hidden_in, grad_out)
    tokens = pl.pallas_call(
        functools.partial(pack_kernel, group_size),
        out_shape=jax.ShapeDtypeStruct((group_count, tok_count, 2 * width + LANES), BF16),
        in_specs=[hbm] * len(own),
        scratch_shapes=[pltpu.VMEM(value.shape, value.dtype) for value in own]
        + [pltpu.SemaphoreType.DMA((len(own),))],
        compiler_params=pltpu.CompilerParams(vmem_limit_bytes=56 * 1024 * 1024),
    )(*own)
    tokens = swap(tokens, "node", across)
    rows = call(
        functools.partial(rows_kernel, routes, slot_cap),
        (group_size, group_count * slot_cap, 2 * width), tokens,
    )
    rows = swap(rows, "node", within).reshape(slot_total, 2 * width)
    main = max(EXTRA, slot_total * 5 // 8 // EXTRA * EXTRA)
    rest_shape = (parts, slot_total - main, 3 * LANES)
    main_sums, rest_sums, place, count = pl.pallas_call(
        parts_kernel,
        out_shape=[
            jax.ShapeDtypeStruct((parts, main, 3 * LANES), BF16),
            jax.ShapeDtypeStruct(rest_shape, BF16),
            jax.ShapeDtypeStruct((slot_total, slot_total), BF16),
            jax.ShapeDtypeStruct((1, 1), jnp.int32),
        ],
        in_specs=[vmem, vmem, hbm, vmem],
        out_specs=[vmem, hbm, vmem, smem],
        scratch_shapes=[
            pltpu.VMEM(w_up.shape, BF16),
            pltpu.VMEM(rest_shape, BF16),
            pltpu.SemaphoreType.DMA((2,)),
        ],
        compiler_params=PARAMS,
    )(rows, w_gate, w_up, w_down)

    def over_local(sums):
        sums = swap(sums, "local")
        hidden = call(hidden_kernel, (parts, sums.shape[1] + TAIL, 2 * LANES), sums)
        return swap(hidden, "local")

    hidden = over_local(main_sums)
    back, count = pl.pallas_call(
        back_kernel,
        out_shape=[
            jax.ShapeDtypeStruct((slot_total, width + LANES), BF16),
            jax.ShapeDtypeStruct((1, 1), jnp.int32),
        ],
        in_specs=[vmem, vmem, vmem, vmem, smem],
        out_specs=[vmem, smem],
        compiler_params=PARAMS,
    )(hidden, w_gate, w_up, place, count)

    def add_rest(back, sums, place, w_gate, w_up):
        return call(rest_kernel, (slot_total, width + LANES), over_local(sums), w_gate, w_up, place, back)

    back = lax.cond(
        count[0, 0] > main, add_rest, lambda back, *_: back, back, rest_sums, place, w_gate, w_up
    )
    back = swap(back.reshape(group_size, group_count * slot_cap, width + LANES), "node", within)
    home = call(
        functools.partial(combine_kernel, routes, slot_cap),
        (group_count, tok_count, width + LANES), tokens, back,
    )
    home = swap(home, "node", across)
    grad_in, scores = call(home_kernel, [(tok_count, width), (routes, tok_count)], home)
    return (grad_in, scores.T)


def solution(mesh):
    return jax.shard_map(
        on_device,
        mesh=mesh,
        in_specs=(
            P("node", "local"),
            P("node", "local"),
            P("node", None),
            P("node", None),
            P("node", "local", None),
            P("node", "local", None),
            P("node", None, "local"),
        ),
        out_specs=(P("node", "local"), P("node", None)),
        check_vma=False,
    )
```

```python
import functools

import jax
import jax.numpy as jnp
from jax import lax
from jax.experimental import pallas as pl
from jax.experimental.pallas import tpu as pltpu
from jax.sharding import PartitionSpec as P

BF16 = jnp.bfloat16
F32 = jnp.float32
EMPTY = 64.0
LANES = 128
EXTRA = 16
TAIL = 8
PARAMS = pltpu.CompilerParams(vmem_limit_bytes=32 * 1024 * 1024)


def dot(left, right, left_dim=1, right_dim=0):
    return lax.dot_general(
        left, right, (((left_dim,), (right_dim,)), ((), ())), preferred_element_type=F32
    )


def iota(shape, dim):
    return lax.broadcasted_iota(jnp.int32, shape, dim)


def split_three(value):
    high = value.astype(BF16)
    rest = value - high.astype(F32)
    middle = rest.astype(BF16)
    return high, middle, (rest - middle.astype(F32)).astype(BF16)


def pack_kernel(size, ids_in, route_in, x_in, y_in, out_ref, ids_ref, route_ref, x_ref, y_ref, sems):
    pairs = ((ids_in, ids_ref), (route_in, route_ref), (x_in, x_ref), (y_in, y_ref))
    copies = [pltpu.make_async_copy(*pair, sems.at[i]) for i, pair in enumerate(pairs)]
    for copy in copies:
        copy.start()
    for copy in copies:
        copy.wait()
    groups, toks, _ = out_ref.shape
    routes = ids_ref.shape[0]
    width = x_ref.shape[1]
    unit = (iota((toks, toks), 0) == iota((toks, toks), 1)).astype(BF16)
    pieces = [piece.astype(F32) for piece in split_three(route_ref[...])]
    fill = jnp.zeros((LANES - 4 * routes, toks), F32)
    for group in range(groups):
        ids = (ids_ref[...] - group * size).astype(F32)
        facts = jnp.concatenate([ids, *pieces, fill], axis=0).astype(BF16)
        out_ref[group, :, :width] = x_ref[...]
        out_ref[group, :, width : 2 * width] = y_ref[...]
        out_ref[group, :, 2 * width :] = dot(unit, facts, 1, 1).astype(BF16)


def route_hits(facts, groups, toks, size, slot_cap, routes):
    shape = (groups * toks, size * groups * slot_cap)
    column = iota(shape, 1)
    expert = column // (groups * slot_cap)
    names = [facts[:, k : k + 1].astype(jnp.int32) == expert for k in range(routes)]
    named = functools.reduce(jnp.logical_or, names)
    square = (groups * toks, groups * toks)
    one, two = iota(square, 0), iota(square, 1)
    before = ((one // toks == two // toks) & (two < one)).astype(BF16)
    earlier = dot(before, named.astype(BF16)).astype(jnp.int32)
    here = (earlier == column % slot_cap) & (
        column // slot_cap % groups == iota(shape, 0) // toks
    )
    return [name & here for name in names], named & here


def rows_kernel(routes, slot_cap, tok_ref, out_ref):
    groups, toks, full = tok_ref.shape
    size = out_ref.shape[0]
    width = full - LANES
    toks_all = tok_ref[...].reshape(groups * toks, full)
    facts = toks_all[:, width:].astype(F32)
    _, taken = route_hits(facts, groups, toks, size, slot_cap, routes)
    taken = taken.astype(F32)
    free = 1.0 - jnp.sum(taken, axis=0, keepdims=True)
    shape = (EXTRA, taken.shape[1])
    free = jnp.where(iota(shape, 0) == 0, jnp.broadcast_to(free, shape), 0.0)
    pick = jnp.concatenate([taken, free], axis=0).astype(BF16)
    rows = jnp.concatenate([toks_all[:, :width], jnp.full((EXTRA, width), EMPTY, BF16)], axis=0)
    picked = dot(pick, rows, 0, 0).astype(BF16)
    out_ref[...] = picked.reshape(out_ref.shape)


def products(x, y, gate_ref, up_ref, down_ref, out_ref):
    parts = out_ref.shape[0]
    for j in range(0, parts, 2):
        step = min(2, parts - j)
        cols = slice(j * LANES, (j + step) * LANES)
        values = (
            dot(x, gate_ref[:, cols]),
            dot(y, down_ref[cols, :], 1, 1),
            dot(x, up_ref[:, cols]),
        )
        for i in range(step):
            for at, value in zip((0, 2, 1), values):
                out_ref[j + i, :, at * LANES : (at + 1) * LANES] = value[
                    :, i * LANES : (i + 1) * LANES
                ].astype(BF16)


def parts_kernel(
    rows_ref, gate_ref, up_in, down_ref, main_ref, rest_out, place_ref, count_ref, up_ref, rest_ref, sems
):
    up_copy = pltpu.make_async_copy(up_in, up_ref, sems.at[0])
    up_copy.start()
    main = main_ref.shape[1]
    slots = rows_ref.shape[0]
    width = gate_ref.shape[0]
    named = rows_ref[:, :LANES].astype(F32)[:, :1] < 0.5 * EMPTY
    named_wide = jnp.broadcast_to(named.astype(F32), (slots, LANES))
    count = jnp.sum(named_wide[:, :1]).astype(jnp.int32)
    count_ref[0, 0] = count
    before = (iota((slots, slots), 1) < iota((slots, slots), 0)).astype(BF16)
    order = dot(before, named_wide.astype(BF16))[:, :1].astype(jnp.int32)
    place = (jnp.where(named, order, slots) == iota((slots, slots), 1)).astype(BF16)
    place_ref[...] = place
    packed = dot(place, rows_ref[...], 0, 0).astype(BF16)
    x, y = packed[:main, :width], packed[:main, width:]
    up_copy.wait()
    products(x, y, gate_ref, up_ref, down_ref, main_ref)

    @pl.when(count > main)
    def _():
        packed = dot(place_ref[...], rows_ref[...], 0, 0).astype(BF16)
        x, y = packed[main:, :width], packed[main:, width:]
        products(x, y, gate_ref, up_ref, down_ref, rest_ref)
        rest_copy = pltpu.make_async_copy(rest_ref, rest_out, sems.at[1])
        rest_copy.start()
        rest_copy.wait()


def hidden_kernel(parts_ref, out_ref):
    parts, rows, _ = parts_ref.shape
    total = parts_ref[0].astype(F32)
    for j in range(1, parts):
        total += parts_ref[j].astype(F32)
    gate_pre = total[:, :LANES]
    up_pre = total[:, LANES : 2 * LANES]
    grad_act = total[:, 2 * LANES :]
    sig = jax.nn.sigmoid(gate_pre)
    silu_val = gate_pre * sig
    product = silu_val * up_pre * grad_act
    grad_gate = (grad_act * up_pre * sig * (1.0 + gate_pre * (1.0 - sig))).astype(BF16)
    grad_up = (grad_act * silu_val).astype(BF16)
    score = lax.dot_general(
        jnp.ones((8, LANES), F32), product, (((1,), (1,)), ((), ())),
        preferred_element_type=F32, precision=lax.Precision.HIGHEST,
    )
    high = score.astype(BF16).astype(F32)
    tail = jnp.where(iota(score.shape, 0) < 4, high, score - high).astype(BF16)
    pad = jnp.zeros((TAIL, 2 * LANES - rows), BF16) if rows < 2 * LANES else None
    if pad is not None:
        tail = jnp.concatenate([tail, pad], axis=1)
    for j in range(parts):
        out_ref[j, :rows, :LANES] = grad_gate
        out_ref[j, :rows, LANES:] = grad_up
        out_ref[j, rows:, :] = tail


def back_rows(hidden_ref, gate_ref, up_ref):
    parts, rows, _ = hidden_ref.shape
    rows -= TAIL
    width = gate_ref.shape[0]
    total = jnp.zeros((rows, width), F32)
    tails = jnp.zeros((TAIL, 2 * LANES), F32)
    for j in range(parts):
        cols = slice(j * LANES, (j + 1) * LANES)
        weights = jnp.concatenate([gate_ref[:, cols], up_ref[:, cols]], axis=1)
        total += dot(hidden_ref[j, :rows, :], weights, 1, 1)
        tails += hidden_ref[j, rows:, :].astype(F32)
    score = jnp.broadcast_to(tails[:1] + tails[4:5], tails.shape).astype(BF16)
    unit = (iota((rows, 2 * LANES), 0) == iota((rows, 2 * LANES), 1)).astype(BF16)
    spread = jnp.concatenate([score] * (LANES // 8), axis=0)
    return total.astype(BF16), dot(unit, spread, 1, 1).astype(BF16)


def back_kernel(hidden_ref, gate_ref, up_ref, place_ref, count_ref, out_ref, count_out):
    count_out[0, 0] = count_ref[0, 0]
    rows = jnp.concatenate(back_rows(hidden_ref, gate_ref, up_ref), axis=1)
    fill = jnp.zeros((place_ref.shape[1] - rows.shape[0], rows.shape[1]), BF16)
    out_ref[...] = dot(place_ref[...], jnp.concatenate([rows, fill], axis=0)).astype(BF16)


def rest_kernel(hidden_ref, gate_ref, up_ref, place_ref, main_ref, out_ref):
    width = gate_ref.shape[0]
    rows, score = back_rows(hidden_ref, gate_ref, up_ref)
    place = place_ref[:, place_ref.shape[1] - rows.shape[0] :]
    out_ref[:, :width] = (main_ref[:, :width].astype(F32) + dot(place, rows)).astype(BF16)
    out_ref[:, width:] = (main_ref[:, width:].astype(F32) + dot(place, score)).astype(BF16)


def combine_kernel(routes, slot_cap, tok_ref, back_ref, out_ref):
    groups, toks, full = tok_ref.shape
    size = back_ref.shape[0]
    width = back_ref.shape[2] - LANES
    facts = tok_ref[:, :, full - LANES :].reshape(groups * toks, LANES).astype(F32)
    back = back_ref[...].reshape(size * groups * slot_cap, width + LANES)
    hits, _ = route_hits(facts, groups, toks, size, slot_cap, routes)
    weight = jnp.zeros(hits[0].shape, F32)
    for k in range(routes):
        value = sum(facts[:, i * routes + k : i * routes + k + 1] for i in (1, 2, 3))
        weight = jnp.where(hits[k], value, weight)
    sums = sum(dot(piece, back[:, :width]) for piece in split_three(weight))
    row = iota((TAIL, groups * toks), 0)
    scores = jnp.zeros((TAIL, groups * toks), F32)
    for k in range(routes):
        found = dot(back[:, width:], hits[k].astype(BF16), 0, 1)
        scores = jnp.where(row == k, found[:TAIL], scores)
    sums = sums.astype(BF16)
    for at in range(0, width, LANES):
        place = at // LANES * toks
        out_ref[:, place : place + toks, :] = sums[:, at : at + LANES].reshape(groups, toks, LANES)
    for group in range(groups):
        own = scores[:, group * toks : (group + 1) * toks]
        own = jnp.concatenate([own, jnp.zeros((TAIL, LANES - toks), F32)], axis=1)
        out_ref[group, width // LANES * toks :, :] = own.astype(BF16)


def home_kernel(parts_ref, grad_ref, score_ref):
    groups = parts_ref.shape[0]
    toks, width = grad_ref.shape
    total = parts_ref[0].astype(F32)
    for group in range(1, groups):
        total += parts_ref[group].astype(F32)
    for at in range(0, width, LANES):
        place = at // LANES * toks
        grad_ref[:, at : at + LANES] = total[place : place + toks].astype(BF16)
    score_ref[...] = total[width // LANES * toks :, :toks].astype(BF16)


def on_device(hidden_in, grad_out, expert_ids, route_weights, gate_weight, up_weight, down_weight):
    node_count = lax.axis_size("node")
    parts = lax.axis_size("local")
    tok_count, width = hidden_in.shape
    group_count = min(8, node_count // 2)
    group_size = node_count // group_count
    slot_cap = 2 * tok_count // group_size
    slot_total = node_count * slot_cap
    routes = expert_ids.shape[1]
    across = [[g * group_size + p for g in range(group_count)] for p in range(group_size)]
    within = [[g * group_size + p for p in range(group_size)] for g in range(group_count)]

    vmem = pl.BlockSpec(memory_space=pltpu.VMEM)
    smem = pl.BlockSpec(memory_space=pltpu.SMEM)
    hbm = pl.BlockSpec(memory_space=pltpu.HBM)

    def swap(value, axis, members=None):
        return lax.all_to_all(
            value, axis, split_axis=0, concat_axis=0, tiled=True, axis_index_groups=members
        )

    w_gate, w_up, w_down = gate_weight[0], up_weight[0], down_weight[0]

    def call(kernel, shape, *args):
        return pl.pallas_call(
            kernel,
            out_shape=jax.tree.map(lambda s: jax.ShapeDtypeStruct(s, BF16), shape, is_leaf=lambda s: isinstance(s, tuple) and isinstance(s[0], int)),
            compiler_params=PARAMS,
        )(*args)

    own = (expert_ids.T, route_weights.T, hidden_in, grad_out)
    tokens = pl.pallas_call(
        functools.partial(pack_kernel, group_size),
        out_shape=jax.ShapeDtypeStruct((group_count, tok_count, 2 * width + LANES), BF16),
        in_specs=[hbm] * len(own),
        scratch_shapes=[pltpu.VMEM(value.shape, value.dtype) for value in own]
        + [pltpu.SemaphoreType.DMA((len(own),))],
        compiler_params=pltpu.CompilerParams(vmem_limit_bytes=56 * 1024 * 1024),
    )(*own)
    tokens = swap(tokens, "node", across)
    rows = call(
        functools.partial(rows_kernel, routes, slot_cap),
        (group_size, group_count * slot_cap, 2 * width), tokens,
    )
    rows = swap(rows, "node", within).reshape(slot_total, 2 * width)
    main = max(EXTRA, slot_total * 5 // 8 // EXTRA * EXTRA)
    rest_shape = (parts, slot_total - main, 3 * LANES)
    main_sums, rest_sums, place, count = pl.pallas_call(
        parts_kernel,
        out_shape=[
            jax.ShapeDtypeStruct((parts, main, 3 * LANES), BF16),
            jax.ShapeDtypeStruct(rest_shape, BF16),
            jax.ShapeDtypeStruct((slot_total, slot_total), BF16),
            jax.ShapeDtypeStruct((1, 1), jnp.int32),
        ],
        in_specs=[vmem, vmem, hbm, vmem],
        out_specs=[vmem, hbm, vmem, smem],
        scratch_shapes=[
            pltpu.VMEM(w_up.shape, BF16),
            pltpu.VMEM(rest_shape, BF16),
            pltpu.SemaphoreType.DMA((2,)),
        ],
        compiler_params=PARAMS,
    )(rows, w_gate, w_up, w_down)

    def over_local(sums):
        sums = swap(sums, "local")
        hidden = call(hidden_kernel, (parts, sums.shape[1] + TAIL, 2 * LANES), sums)
        return swap(hidden, "local")

    hidden = over_local(main_sums)
    back, count = pl.pallas_call(
        back_kernel,
        out_shape=[
            jax.ShapeDtypeStruct((slot_total, width + LANES), BF16),
            jax.ShapeDtypeStruct((1, 1), jnp.int32),
        ],
        in_specs=[vmem, vmem, vmem, vmem, smem],
        out_specs=[vmem, smem],
        compiler_params=PARAMS,
    )(hidden, w_gate, w_up, place, count)

    def add_rest(back, sums, place, w_gate, w_up):
        return call(rest_kernel, (slot_total, width + LANES), over_local(sums), w_gate, w_up, place, back)

    back = lax.cond(
        count[0, 0] > main, add_rest, lambda back, *_: back, back, rest_sums, place, w_gate, w_up
    )
    back = swap(back.reshape(group_size, group_count * slot_cap, width + LANES), "node", within)
    home = call(
        functools.partial(combine_kernel, routes, slot_cap),
        (group_count, width // LANES * tok_count + TAIL, LANES), tokens, back,
    )
    home = swap(home, "node", across)
    grad_in, scores = call(home_kernel, [(tok_count, width), (routes, tok_count)], home)
    return (grad_in, scores.T)


def solution(mesh):
    return jax.shard_map(
        on_device,
        mesh=mesh,
        in_specs=(
            P("node", "local"),
            P("node", "local"),
            P("node", None),
            P("node", None),
            P("node", "local", None),
            P("node", "local", None),
            P("node", None, "local"),
        ),
        out_specs=(P("node", "local"), P("node", None)),
        check_vma=False,
    )
```

```python
import functools

import jax
import jax.numpy as jnp
from jax import lax
from jax.experimental import pallas as pl
from jax.experimental.pallas import tpu as pltpu
from jax.sharding import PartitionSpec as P

BF16 = jnp.bfloat16
F32 = jnp.float32
EMPTY = 64.0
LANES = 128
EXTRA = 16
TAIL = 8
PARAMS = pltpu.CompilerParams(vmem_limit_bytes=32 * 1024 * 1024)


def dot(left, right, left_dim=1, right_dim=0):
    return lax.dot_general(
        left, right, (((left_dim,), (right_dim,)), ((), ())), preferred_element_type=F32
    )


def iota(shape, dim):
    return lax.broadcasted_iota(jnp.int32, shape, dim)


def split_three(value):
    high = value.astype(BF16)
    rest = value - high.astype(F32)
    middle = rest.astype(BF16)
    return high, middle, (rest - middle.astype(F32)).astype(BF16)


def pack_kernel(size, ids_in, route_in, x_in, y_in, out_ref, ids_ref, route_ref, x_ref, y_ref, sems):
    pairs = ((ids_in, ids_ref), (route_in, route_ref), (x_in, x_ref), (y_in, y_ref))
    copies = [pltpu.make_async_copy(*pair, sems.at[i]) for i, pair in enumerate(pairs)]
    for copy in copies:
        copy.start()
    for copy in copies:
        copy.wait()
    groups, toks, _ = out_ref.shape
    routes = ids_ref.shape[0]
    width = x_ref.shape[1]
    unit = (iota((toks, toks), 0) == iota((toks, toks), 1)).astype(BF16)
    pieces = [piece.astype(F32) for piece in split_three(route_ref[...])]
    fill = jnp.zeros((LANES - 4 * routes, toks), F32)
    for group in range(groups):
        ids = (ids_ref[...] - group * size).astype(F32)
        facts = jnp.concatenate([ids, *pieces, fill], axis=0).astype(BF16)
        out_ref[group, :, :width] = x_ref[...]
        out_ref[group, :, width : 2 * width] = y_ref[...]
        out_ref[group, :, 2 * width :] = dot(unit, facts, 1, 1).astype(BF16)


def route_hits(facts, groups, toks, size, slot_cap, routes):
    shape = (groups * toks, size * groups * slot_cap)
    column = iota(shape, 1)
    expert = column // (groups * slot_cap)
    names = [facts[:, k : k + 1].astype(jnp.int32) == expert for k in range(routes)]
    named = functools.reduce(jnp.logical_or, names)
    square = (groups * toks, groups * toks)
    one, two = iota(square, 0), iota(square, 1)
    before = ((one // toks == two // toks) & (two < one)).astype(BF16)
    earlier = dot(before, named.astype(BF16)).astype(jnp.int32)
    here = (earlier == column % slot_cap) & (
        column // slot_cap % groups == iota(shape, 0) // toks
    )
    return [name & here for name in names], named & here


def rows_kernel(routes, slot_cap, tok_ref, out_ref):
    groups, toks, full = tok_ref.shape
    size = out_ref.shape[0]
    width = full - LANES
    toks_all = tok_ref[...].reshape(groups * toks, full)
    facts = toks_all[:, width:].astype(F32)
    _, taken = route_hits(facts, groups, toks, size, slot_cap, routes)
    taken = taken.astype(F32)
    free = 1.0 - jnp.sum(taken, axis=0, keepdims=True)
    shape = (EXTRA, taken.shape[1])
    free = jnp.where(iota(shape, 0) == 0, jnp.broadcast_to(free, shape), 0.0)
    pick = jnp.concatenate([taken, free], axis=0).astype(BF16)
    rows = jnp.concatenate([toks_all[:, :width], jnp.full((EXTRA, width), EMPTY, BF16)], axis=0)
    picked = dot(pick, rows, 0, 0).astype(BF16)
    out_ref[...] = picked.reshape(out_ref.shape)


def products(x, y, gate_ref, up_ref, down_ref, out_ref):
    parts = out_ref.shape[0]
    for j in range(0, parts, 2):
        step = min(2, parts - j)
        cols = slice(j * LANES, (j + step) * LANES)
        values = (
            dot(x, gate_ref[:, cols]),
            dot(y, down_ref[cols, :], 1, 1),
            dot(x, up_ref[:, cols]),
        )
        for i in range(step):
            for at, value in zip((0, 2, 1), values):
                out_ref[j + i, :, at * LANES : (at + 1) * LANES] = value[
                    :, i * LANES : (i + 1) * LANES
                ].astype(BF16)


def parts_kernel(
    rows_ref, gate_ref, up_in, down_ref, main_ref, rest_out, place_ref, count_ref, up_ref, rest_ref, sems
):
    up_copy = pltpu.make_async_copy(up_in, up_ref, sems.at[0])
    up_copy.start()
    main = main_ref.shape[1]
    slots = rows_ref.shape[0]
    width = gate_ref.shape[0]
    named = rows_ref[:, :LANES].astype(F32)[:, :1] < 0.5 * EMPTY
    named_wide = jnp.broadcast_to(named.astype(F32), (slots, LANES))
    count = jnp.sum(named_wide[:, :1]).astype(jnp.int32)
    count_ref[0, 0] = count
    before = (iota((slots, slots), 1) < iota((slots, slots), 0)).astype(BF16)
    order = dot(before, named_wide.astype(BF16))[:, :1].astype(jnp.int32)
    place = (jnp.where(named, order, slots) == iota((slots, slots), 1)).astype(BF16)
    place_ref[...] = place
    packed = dot(place, rows_ref[...], 0, 0).astype(BF16)
    x, y = packed[:main, :width], packed[:main, width:]
    up_copy.wait()
    products(x, y, gate_ref, up_ref, down_ref, main_ref)

    @pl.when(count > main)
    def _():
        packed = dot(place_ref[...], rows_ref[...], 0, 0).astype(BF16)
        x, y = packed[main:, :width], packed[main:, width:]
        products(x, y, gate_ref, up_ref, down_ref, rest_ref)
        rest_copy = pltpu.make_async_copy(rest_ref, rest_out, sems.at[1])
        rest_copy.start()
        rest_copy.wait()


def hidden_kernel(parts_ref, out_ref):
    parts, rows, _ = parts_ref.shape
    total = parts_ref[0].astype(F32)
    for j in range(1, parts):
        total += parts_ref[j].astype(F32)
    gate_pre = total[:, :LANES]
    up_pre = total[:, LANES : 2 * LANES]
    grad_act = total[:, 2 * LANES :]
    sig = jax.nn.sigmoid(gate_pre)
    silu_val = gate_pre * sig
    product = silu_val * up_pre * grad_act
    grad_gate = (grad_act * up_pre * sig * (1.0 + gate_pre * (1.0 - sig))).astype(BF16)
    grad_up = (grad_act * silu_val).astype(BF16)
    score = lax.dot_general(
        jnp.ones((8, LANES), F32), product, (((1,), (1,)), ((), ())),
        preferred_element_type=F32, precision=lax.Precision.HIGHEST,
    )
    high = score.astype(BF16).astype(F32)
    tail = jnp.where(iota(score.shape, 0) < 4, high, score - high).astype(BF16)
    pad = jnp.zeros((TAIL, 2 * LANES - rows), BF16) if rows < 2 * LANES else None
    if pad is not None:
        tail = jnp.concatenate([tail, pad], axis=1)
    for j in range(parts):
        out_ref[j, :rows, :LANES] = grad_gate
        out_ref[j, :rows, LANES:] = grad_up
        out_ref[j, rows:, :] = tail


def back_rows(hidden_ref, gate_ref, up_ref):
    parts, rows, _ = hidden_ref.shape
    rows -= TAIL
    width = gate_ref.shape[0]
    total = jnp.zeros((rows, width), F32)
    tails = jnp.zeros((TAIL, 2 * LANES), F32)
    for j in range(parts):
        cols = slice(j * LANES, (j + 1) * LANES)
        weights = jnp.concatenate([gate_ref[:, cols], up_ref[:, cols]], axis=1)
        total += dot(hidden_ref[j, :rows, :], weights, 1, 1)
        tails += hidden_ref[j, rows:, :].astype(F32)
    score = jnp.broadcast_to(tails[:1] + tails[4:5], tails.shape).astype(BF16)
    return total.astype(BF16), score


def put_back(moved, scores, out_ref):
    places, _, _ = out_ref.shape
    slots, width = moved.shape
    each = slots // places
    for at in range(0, width, LANES):
        start = at // LANES * each
        out_ref[:, start : start + each, :] = moved[:, at : at + LANES].astype(BF16).reshape(
            places, each, LANES
        )
    for place in range(places):
        own = scores[:, place * each : (place + 1) * each]
        own = jnp.concatenate([own, jnp.zeros((TAIL, LANES - each), F32)], axis=1)
        out_ref[place, width // LANES * each :, :] = own.astype(BF16)


def read_back(back_ref, width):
    places, height, _ = back_ref.shape
    each = (height - TAIL) * LANES // width
    pieces = [
        back_ref[:, start : start + each, :].reshape(places * each, LANES)
        for start in range(0, height - TAIL, each)
    ]
    tails = back_ref[:, height - TAIL :, :].astype(F32).reshape(places * TAIL, LANES)
    shape = (LANES, places * each)
    spread = dot(tails.astype(BF16), (iota(shape, 0) == iota(shape, 1) % each).astype(BF16))
    row, column = iota(spread.shape, 0), iota(spread.shape, 1)
    scores = jnp.sum(jnp.where(row == column // each * TAIL, spread, 0.0), axis=0, keepdims=True)
    return jnp.concatenate(pieces, axis=1), jnp.broadcast_to(scores, (TAIL, scores.shape[1]))


def back_kernel(hidden_ref, gate_ref, up_ref, place_ref, count_ref, out_ref, count_out):
    count_out[0, 0] = count_ref[0, 0]
    rows, score = back_rows(hidden_ref, gate_ref, up_ref)
    fill = jnp.zeros((place_ref.shape[1] - rows.shape[0], rows.shape[1]), BF16)
    moved = dot(place_ref[...], jnp.concatenate([rows, fill], axis=0))
    put_back(moved, dot(score, place_ref[...], 1, 1), out_ref)


def rest_kernel(hidden_ref, gate_ref, up_ref, place_ref, main_ref, out_ref):
    rows, score = back_rows(hidden_ref, gate_ref, up_ref)
    last = place_ref[:, place_ref.shape[1] - rows.shape[0] :]
    main, main_scores = read_back(main_ref, rows.shape[1])
    moved = main.astype(F32) + dot(last, rows)
    put_back(moved, main_scores + dot(score[:, : rows.shape[0]], last, 1, 1), out_ref)


def combine_kernel(routes, slot_cap, tok_ref, back_ref, out_ref):
    groups, toks, full = tok_ref.shape
    size = back_ref.shape[0]
    width = (full - LANES) // 2
    facts = tok_ref[:, :, full - LANES :].reshape(groups * toks, LANES).astype(F32)
    back, slot_scores = read_back(back_ref, width)
    slot_scores = slot_scores.astype(BF16)
    hits, _ = route_hits(facts, groups, toks, size, slot_cap, routes)
    weight = jnp.zeros(hits[0].shape, F32)
    for k in range(routes):
        value = sum(facts[:, i * routes + k : i * routes + k + 1] for i in (1, 2, 3))
        weight = jnp.where(hits[k], value, weight)
    sums = sum(dot(piece, back) for piece in split_three(weight))
    row = iota((TAIL, groups * toks), 0)
    scores = jnp.zeros((TAIL, groups * toks), F32)
    for k in range(routes):
        found = dot(slot_scores, hits[k].astype(BF16), 1, 1)
        scores = jnp.where(row == k, found, scores)
    sums = sums.astype(BF16)
    for at in range(0, width, LANES):
        place = at // LANES * toks
        out_ref[:, place : place + toks, :] = sums[:, at : at + LANES].reshape(groups, toks, LANES)
    for group in range(groups):
        own = scores[:, group * toks : (group + 1) * toks]
        own = jnp.concatenate([own, jnp.zeros((TAIL, LANES - toks), F32)], axis=1)
        out_ref[group, width // LANES * toks :, :] = own.astype(BF16)


def home_kernel(parts_ref, grad_ref, score_ref):
    groups = parts_ref.shape[0]
    toks, width = grad_ref.shape
    total = parts_ref[0].astype(F32)
    for group in range(1, groups):
        total += parts_ref[group].astype(F32)
    for at in range(0, width, LANES):
        place = at // LANES * toks
        grad_ref[:, at : at + LANES] = total[place : place + toks].astype(BF16)
    score_ref[...] = total[width // LANES * toks :, :toks].astype(BF16)


def on_device(hidden_in, grad_out, expert_ids, route_weights, gate_weight, up_weight, down_weight):
    node_count = lax.axis_size("node")
    parts = lax.axis_size("local")
    tok_count, width = hidden_in.shape
    group_count = min(8, node_count // 2)
    group_size = node_count // group_count
    slot_cap = 2 * tok_count // group_size
    slot_total = node_count * slot_cap
    routes = expert_ids.shape[1]
    across = [[g * group_size + p for g in range(group_count)] for p in range(group_size)]
    within = [[g * group_size + p for p in range(group_size)] for g in range(group_count)]

    vmem = pl.BlockSpec(memory_space=pltpu.VMEM)
    smem = pl.BlockSpec(memory_space=pltpu.SMEM)
    hbm = pl.BlockSpec(memory_space=pltpu.HBM)

    def swap(value, axis, members=None):
        return lax.all_to_all(
            value, axis, split_axis=0, concat_axis=0, tiled=True, axis_index_groups=members
        )

    w_gate, w_up, w_down = gate_weight[0], up_weight[0], down_weight[0]

    def call(kernel, shape, *args):
        return pl.pallas_call(
            kernel,
            out_shape=jax.tree.map(lambda s: jax.ShapeDtypeStruct(s, BF16), shape, is_leaf=lambda s: isinstance(s, tuple) and isinstance(s[0], int)),
            compiler_params=PARAMS,
        )(*args)

    own = (expert_ids.T, route_weights.T, hidden_in, grad_out)
    tokens = pl.pallas_call(
        functools.partial(pack_kernel, group_size),
        out_shape=jax.ShapeDtypeStruct((group_count, tok_count, 2 * width + LANES), BF16),
        in_specs=[hbm] * len(own),
        scratch_shapes=[pltpu.VMEM(value.shape, value.dtype) for value in own]
        + [pltpu.SemaphoreType.DMA((len(own),))],
        compiler_params=pltpu.CompilerParams(vmem_limit_bytes=56 * 1024 * 1024),
    )(*own)
    tokens = swap(tokens, "node", across)
    rows = call(
        functools.partial(rows_kernel, routes, slot_cap),
        (group_size, group_count * slot_cap, 2 * width), tokens,
    )
    rows = swap(rows, "node", within).reshape(slot_total, 2 * width)
    main = max(EXTRA, slot_total * 5 // 8 // EXTRA * EXTRA)
    rest_shape = (parts, slot_total - main, 3 * LANES)
    main_sums, rest_sums, place, count = pl.pallas_call(
        parts_kernel,
        out_shape=[
            jax.ShapeDtypeStruct((parts, main, 3 * LANES), BF16),
            jax.ShapeDtypeStruct(rest_shape, BF16),
            jax.ShapeDtypeStruct((slot_total, slot_total), BF16),
            jax.ShapeDtypeStruct((1, 1), jnp.int32),
        ],
        in_specs=[vmem, vmem, hbm, vmem],
        out_specs=[vmem, hbm, vmem, smem],
        scratch_shapes=[
            pltpu.VMEM(w_up.shape, BF16),
            pltpu.VMEM(rest_shape, BF16),
            pltpu.SemaphoreType.DMA((2,)),
        ],
        compiler_params=PARAMS,
    )(rows, w_gate, w_up, w_down)

    def over_local(sums):
        sums = swap(sums, "local")
        hidden = call(hidden_kernel, (parts, sums.shape[1] + TAIL, 2 * LANES), sums)
        return swap(hidden, "local")

    hidden = over_local(main_sums)
    each = group_count * slot_cap
    back_shape = (group_size, width // LANES * each + TAIL, LANES)
    back, count = pl.pallas_call(
        back_kernel,
        out_shape=[
            jax.ShapeDtypeStruct(back_shape, BF16),
            jax.ShapeDtypeStruct((1, 1), jnp.int32),
        ],
        in_specs=[vmem, vmem, vmem, vmem, smem],
        out_specs=[vmem, smem],
        compiler_params=PARAMS,
    )(hidden, w_gate, w_up, place, count)

    def add_rest(back, sums, place, w_gate, w_up):
        return call(rest_kernel, back_shape, over_local(sums), w_gate, w_up, place, back)

    back = lax.cond(
        count[0, 0] > main, add_rest, lambda back, *_: back, back, rest_sums, place, w_gate, w_up
    )
    back = swap(back, "node", within)
    home = call(
        functools.partial(combine_kernel, routes, slot_cap),
        (group_count, width // LANES * tok_count + TAIL, LANES), tokens, back,
    )
    home = swap(home, "node", across)
    grad_in, scores = call(home_kernel, [(tok_count, width), (routes, tok_count)], home)
    return (grad_in, scores.T)


def solution(mesh):
    return jax.shard_map(
        on_device,
        mesh=mesh,
        in_specs=(
            P("node", "local"),
            P("node", "local"),
            P("node", None),
            P("node", None),
            P("node", "local", None),
            P("node", "local", None),
            P("node", None, "local"),
        ),
        out_specs=(P("node", "local"), P("node", None)),
        check_vma=False,
    )
```

```python
import functools

import jax
import jax.numpy as jnp
from jax import lax
from jax.experimental import pallas as pl
from jax.experimental.pallas import tpu as pltpu
from jax.sharding import PartitionSpec as P

BF16 = jnp.bfloat16
F32 = jnp.float32
EMPTY = 64.0
LANES = 128
EXTRA = 16
TAIL = 8
PARAMS = pltpu.CompilerParams(vmem_limit_bytes=32 * 1024 * 1024)


def dot(left, right, left_dim=1, right_dim=0):
    return lax.dot_general(
        left, right, (((left_dim,), (right_dim,)), ((), ())), preferred_element_type=F32
    )


def iota(shape, dim):
    return lax.broadcasted_iota(jnp.int32, shape, dim)


def split_three(value):
    high = value.astype(BF16)
    rest = value - high.astype(F32)
    middle = rest.astype(BF16)
    return high, middle, (rest - middle.astype(F32)).astype(BF16)


def pack_kernel(size, ids_in, route_in, x_in, y_in, out_ref, ids_ref, route_ref, x_ref, y_ref, sems):
    pairs = ((ids_in, ids_ref), (route_in, route_ref), (x_in, x_ref), (y_in, y_ref))
    copies = [pltpu.make_async_copy(*pair, sems.at[i]) for i, pair in enumerate(pairs)]
    for copy in copies:
        copy.start()
    groups, toks, _ = out_ref.shape
    routes = ids_ref.shape[0]
    width = x_ref.shape[1]
    unit = (iota((toks, toks), 0) == iota((toks, toks), 1)).astype(BF16)
    copies[0].wait()
    copies[1].wait()
    pieces = [piece.astype(F32) for piece in split_three(route_ref[...])]
    fill = jnp.zeros((LANES - 4 * routes, toks), F32)
    facts = jnp.concatenate([ids_ref[...].astype(F32), *pieces, fill], axis=0).astype(BF16)
    facts = dot(unit, facts, 1, 1)
    names = iota(facts.shape, 1) < routes
    copies[2].wait()
    copies[3].wait()
    for group in range(groups):
        out_ref[group, :, :width] = x_ref[...]
        out_ref[group, :, width : 2 * width] = y_ref[...]
        out_ref[group, :, 2 * width :] = jnp.where(names, facts - group * size, facts).astype(BF16)


def route_hits(facts, groups, toks, size, slot_cap, routes):
    shape = (groups * toks, size * groups * slot_cap)
    column = iota(shape, 1)
    expert = column // (groups * slot_cap)
    names = [facts[:, k : k + 1].astype(jnp.int32) == expert for k in range(routes)]
    named = functools.reduce(jnp.logical_or, names)
    square = (groups * toks, groups * toks)
    one, two = iota(square, 0), iota(square, 1)
    before = ((one // toks == two // toks) & (two < one)).astype(BF16)
    earlier = dot(before, named.astype(BF16)).astype(jnp.int32)
    here = (earlier == column % slot_cap) & (
        column // slot_cap % groups == iota(shape, 0) // toks
    )
    return [name & here for name in names], named & here


def rows_kernel(routes, slot_cap, tok_ref, out_ref):
    groups, toks, full = tok_ref.shape
    size = out_ref.shape[0]
    width = full - LANES
    toks_all = tok_ref[...].reshape(groups * toks, full)
    facts = toks_all[:, width:].astype(F32)
    _, taken = route_hits(facts, groups, toks, size, slot_cap, routes)
    taken = taken.astype(F32)
    free = 1.0 - jnp.sum(taken, axis=0, keepdims=True)
    shape = (EXTRA, taken.shape[1])
    free = jnp.where(iota(shape, 0) == 0, jnp.broadcast_to(free, shape), 0.0)
    pick = jnp.concatenate([taken, free], axis=0).astype(BF16)
    rows = jnp.concatenate([toks_all[:, :width], jnp.full((EXTRA, width), EMPTY, BF16)], axis=0)
    picked = dot(pick, rows, 0, 0).astype(BF16)
    out_ref[...] = picked.reshape(out_ref.shape)


def products(x, y, gate_ref, up_ref, down_ref, out_ref):
    parts = out_ref.shape[0]
    for j in range(0, parts, 2):
        step = min(2, parts - j)
        cols = slice(j * LANES, (j + step) * LANES)
        values = (
            dot(x, gate_ref[:, cols]),
            dot(y, down_ref[cols, :], 1, 1),
            dot(x, up_ref[:, cols]),
        )
        for i in range(step):
            for at, value in zip((0, 2, 1), values):
                out_ref[j + i, :, at * LANES : (at + 1) * LANES] = value[
                    :, i * LANES : (i + 1) * LANES
                ].astype(BF16)


def parts_kernel(
    rows_ref, gate_ref, up_in, down_ref, main_ref, rest_out, place_ref, count_ref, up_ref, rest_ref, sems
):
    up_copy = pltpu.make_async_copy(up_in, up_ref, sems.at[0])
    up_copy.start()
    main = main_ref.shape[1]
    slots = rows_ref.shape[0]
    width = gate_ref.shape[0]
    named = rows_ref[:, :LANES].astype(F32)[:, :1] < 0.5 * EMPTY
    named_wide = jnp.broadcast_to(named.astype(F32), (slots, LANES))
    count = jnp.sum(named_wide[:, :1]).astype(jnp.int32)
    count_ref[0, 0] = count
    before = (iota((slots, slots), 1) < iota((slots, slots), 0)).astype(BF16)
    order = dot(before, named_wide.astype(BF16))[:, :1].astype(jnp.int32)
    place = (jnp.where(named, order, slots) == iota((slots, slots), 1)).astype(BF16)
    place_ref[...] = place
    packed = dot(place, rows_ref[...], 0, 0).astype(BF16)
    x, y = packed[:main, :width], packed[:main, width:]
    up_copy.wait()
    products(x, y, gate_ref, up_ref, down_ref, main_ref)

    @pl.when(count > main)
    def _():
        packed = dot(place_ref[...], rows_ref[...], 0, 0).astype(BF16)
        x, y = packed[main:, :width], packed[main:, width:]
        products(x, y, gate_ref, up_ref, down_ref, rest_ref)
        rest_copy = pltpu.make_async_copy(rest_ref, rest_out, sems.at[1])
        rest_copy.start()
        rest_copy.wait()


def hidden_kernel(parts_ref, out_ref):
    parts, rows, _ = parts_ref.shape
    total = parts_ref[0].astype(F32)
    for j in range(1, parts):
        total += parts_ref[j].astype(F32)
    gate_pre = total[:, :LANES]
    up_pre = total[:, LANES : 2 * LANES]
    grad_act = total[:, 2 * LANES :]
    sig = jax.nn.sigmoid(gate_pre)
    silu_val = gate_pre * sig
    product = silu_val * up_pre * grad_act
    grad_gate = (grad_act * up_pre * sig * (1.0 + gate_pre * (1.0 - sig))).astype(BF16)
    grad_up = (grad_act * silu_val).astype(BF16)
    score = lax.dot_general(
        jnp.ones((8, LANES), F32), product, (((1,), (1,)), ((), ())),
        preferred_element_type=F32, precision=lax.Precision.HIGHEST,
    )
    high = score.astype(BF16).astype(F32)
    tail = jnp.where(iota(score.shape, 0) < 4, high, score - high).astype(BF16)
    pad = jnp.zeros((TAIL, 2 * LANES - rows), BF16) if rows < 2 * LANES else None
    if pad is not None:
        tail = jnp.concatenate([tail, pad], axis=1)
    for j in range(parts):
        out_ref[j, :rows, :LANES] = grad_gate
        out_ref[j, :rows, LANES:] = grad_up
        out_ref[j, rows:, :] = tail


def back_rows(hidden_ref, gate_ref, up_ref):
    parts, rows, _ = hidden_ref.shape
    rows -= TAIL
    width = gate_ref.shape[0]
    total = jnp.zeros((rows, width), F32)
    tails = jnp.zeros((TAIL, 2 * LANES), F32)
    for j in range(parts):
        cols = slice(j * LANES, (j + 1) * LANES)
        weights = jnp.concatenate([gate_ref[:, cols], up_ref[:, cols]], axis=1)
        total += dot(hidden_ref[j, :rows, :], weights, 1, 1)
        tails += hidden_ref[j, rows:, :].astype(F32)
    score = jnp.broadcast_to(tails[:1] + tails[4:5], tails.shape).astype(BF16)
    unit = (iota((rows, 2 * LANES), 0) == iota((rows, 2 * LANES), 1)).astype(BF16)
    spread = jnp.concatenate([score] * (LANES // 8), axis=0)
    return total.astype(BF16), dot(unit, spread, 1, 1).astype(BF16)


def back_kernel(hidden_ref, gate_ref, up_ref, place_ref, count_ref, out_ref, count_out):
    count_out[0, 0] = count_ref[0, 0]
    rows = jnp.concatenate(back_rows(hidden_ref, gate_ref, up_ref), axis=1)
    fill = jnp.zeros((place_ref.shape[1] - rows.shape[0], rows.shape[1]), BF16)
    out_ref[...] = dot(place_ref[...], jnp.concatenate([rows, fill], axis=0)).astype(BF16)


def rest_kernel(hidden_ref, gate_ref, up_ref, place_ref, main_ref, out_ref):
    width = gate_ref.shape[0]
    rows, score = back_rows(hidden_ref, gate_ref, up_ref)
    place = place_ref[:, place_ref.shape[1] - rows.shape[0] :]
    out_ref[:, :width] = (main_ref[:, :width].astype(F32) + dot(place, rows)).astype(BF16)
    out_ref[:, width:] = (main_ref[:, width:].astype(F32) + dot(place, score)).astype(BF16)


def combine_kernel(routes, slot_cap, tok_ref, back_ref, out_ref):
    groups, toks, full = tok_ref.shape
    size = back_ref.shape[0]
    width = back_ref.shape[2] - LANES
    facts = tok_ref[:, :, full - LANES :].reshape(groups * toks, LANES).astype(F32)
    back = back_ref[...].reshape(size * groups * slot_cap, width + LANES)
    hits, _ = route_hits(facts, groups, toks, size, slot_cap, routes)
    weight = jnp.zeros(hits[0].shape, F32)
    for k in range(routes):
        value = sum(facts[:, i * routes + k : i * routes + k + 1] for i in (1, 2, 3))
        weight = jnp.where(hits[k], value, weight)
    sums = sum(dot(piece, back[:, :width]) for piece in split_three(weight))
    row = iota((TAIL, groups * toks), 0)
    scores = jnp.zeros((TAIL, groups * toks), F32)
    for k in range(routes):
        found = dot(back[:, width:], hits[k].astype(BF16), 0, 1)
        scores = jnp.where(row == k, found[:TAIL], scores)
    sums = sums.astype(BF16)
    for at in range(0, width, LANES):
        place = at // LANES * toks
        out_ref[:, place : place + toks, :] = sums[:, at : at + LANES].reshape(groups, toks, LANES)
    for group in range(groups):
        own = scores[:, group * toks : (group + 1) * toks]
        own = jnp.concatenate([own, jnp.zeros((TAIL, LANES - toks), F32)], axis=1)
        out_ref[group, width // LANES * toks :, :] = own.astype(BF16)


def home_kernel(parts_ref, grad_ref, score_ref):
    groups = parts_ref.shape[0]
    toks, width = grad_ref.shape
    total = parts_ref[0].astype(F32)
    for group in range(1, groups):
        total += parts_ref[group].astype(F32)
    for at in range(0, width, LANES):
        place = at // LANES * toks
        grad_ref[:, at : at + LANES] = total[place : place + toks].astype(BF16)
    score_ref[...] = total[width // LANES * toks :, :toks].astype(BF16)


def on_device(hidden_in, grad_out, expert_ids, route_weights, gate_weight, up_weight, down_weight):
    node_count = lax.axis_size("node")
    parts = lax.axis_size("local")
    tok_count, width = hidden_in.shape
    group_count = min(8, node_count // 2)
    group_size = node_count // group_count
    slot_cap = 2 * tok_count // group_size
    slot_total = node_count * slot_cap
    routes = expert_ids.shape[1]
    across = [[g * group_size + p for g in range(group_count)] for p in range(group_size)]
    within = [[g * group_size + p for p in range(group_size)] for g in range(group_count)]

    vmem = pl.BlockSpec(memory_space=pltpu.VMEM)
    smem = pl.BlockSpec(memory_space=pltpu.SMEM)
    hbm = pl.BlockSpec(memory_space=pltpu.HBM)

    def swap(value, axis, members=None):
        return lax.all_to_all(
            value, axis, split_axis=0, concat_axis=0, tiled=True, axis_index_groups=members
        )

    w_gate, w_up, w_down = gate_weight[0], up_weight[0], down_weight[0]

    def call(kernel, shape, *args):
        return pl.pallas_call(
            kernel,
            out_shape=jax.tree.map(lambda s: jax.ShapeDtypeStruct(s, BF16), shape, is_leaf=lambda s: isinstance(s, tuple) and isinstance(s[0], int)),
            compiler_params=PARAMS,
        )(*args)

    own = (expert_ids.T, route_weights.T, hidden_in, grad_out)
    tokens = pl.pallas_call(
        functools.partial(pack_kernel, group_size),
        out_shape=jax.ShapeDtypeStruct((group_count, tok_count, 2 * width + LANES), BF16),
        in_specs=[hbm] * len(own),
        scratch_shapes=[pltpu.VMEM(value.shape, value.dtype) for value in own]
        + [pltpu.SemaphoreType.DMA((len(own),))],
        compiler_params=pltpu.CompilerParams(vmem_limit_bytes=56 * 1024 * 1024),
    )(*own)
    tokens = swap(tokens, "node", across)
    rows = call(
        functools.partial(rows_kernel, routes, slot_cap),
        (group_size, group_count * slot_cap, 2 * width), tokens,
    )
    rows = swap(rows, "node", within).reshape(slot_total, 2 * width)
    main = max(EXTRA, slot_total * 5 // 8 // EXTRA * EXTRA)
    rest_shape = (parts, slot_total - main, 3 * LANES)
    main_sums, rest_sums, place, count = pl.pallas_call(
        parts_kernel,
        out_shape=[
            jax.ShapeDtypeStruct((parts, main, 3 * LANES), BF16),
            jax.ShapeDtypeStruct(rest_shape, BF16),
            jax.ShapeDtypeStruct((slot_total, slot_total), BF16),
            jax.ShapeDtypeStruct((1, 1), jnp.int32),
        ],
        in_specs=[vmem, vmem, hbm, vmem],
        out_specs=[vmem, hbm, vmem, smem],
        scratch_shapes=[
            pltpu.VMEM(w_up.shape, BF16),
            pltpu.VMEM(rest_shape, BF16),
            pltpu.SemaphoreType.DMA((2,)),
        ],
        compiler_params=PARAMS,
    )(rows, w_gate, w_up, w_down)

    def over_local(sums):
        sums = swap(sums, "local")
        hidden = call(hidden_kernel, (parts, sums.shape[1] + TAIL, 2 * LANES), sums)
        return swap(hidden, "local")

    hidden = over_local(main_sums)
    back, count = pl.pallas_call(
        back_kernel,
        out_shape=[
            jax.ShapeDtypeStruct((slot_total, width + LANES), BF16),
            jax.ShapeDtypeStruct((1, 1), jnp.int32),
        ],
        in_specs=[vmem, vmem, vmem, vmem, smem],
        out_specs=[vmem, smem],
        compiler_params=PARAMS,
    )(hidden, w_gate, w_up, place, count)

    def add_rest(back, sums, place, w_gate, w_up):
        return call(rest_kernel, (slot_total, width + LANES), over_local(sums), w_gate, w_up, place, back)

    back = lax.cond(
        count[0, 0] > main, add_rest, lambda back, *_: back, back, rest_sums, place, w_gate, w_up
    )
    back = swap(back.reshape(group_size, group_count * slot_cap, width + LANES), "node", within)
    home = call(
        functools.partial(combine_kernel, routes, slot_cap),
        (group_count, width // LANES * tok_count + TAIL, LANES), tokens, back,
    )
    home = swap(home, "node", across)
    grad_in, scores = call(home_kernel, [(tok_count, width), (routes, tok_count)], home)
    return (grad_in, scores.T)


def solution(mesh):
    return jax.shard_map(
        on_device,
        mesh=mesh,
        in_specs=(
            P("node", "local"),
            P("node", "local"),
            P("node", None),
            P("node", None),
            P("node", "local", None),
            P("node", "local", None),
            P("node", None, "local"),
        ),
        out_specs=(P("node", "local"), P("node", None)),
        check_vma=False,
    )
```
